32 devices in a mesh: dp: 4 (over y, x), seq: 8 (over z, core).
Axes of the slice: x: 2, y: 2, z: 4, core: 2. Of those that a mesh axis runs over, the one named last changes fastest.
Arguments:
- queries: bfloat16 [4096, 1152], P(('dp', 'seq')), may hold values from -6 to 6
- keys: bfloat16 [4096, 1152], P(('dp', 'seq')), may hold values from -6 to 6
- values: bfloat16 [4096, 1152], P(('dp', 'seq')), may hold values from -6 to 6
- out_grad: bfloat16 [4096, 1152], P(('dp', 'seq')), may hold values from -6 to 6
- out_weight: bfloat16 [1152, 1152], replicated, may hold values from -0.1875 to 0.1875
- extents: int32 [4, 8], P('dp'), may hold values from 1 to 8, 16 in all within a row
Outputs:
- query_grad: bfloat16 [4096, 1152], P(('dp', 'seq'))
- key_grad: bfloat16 [4096, 1152], P(('dp', 'seq'))
- value_grad: bfloat16 [4096, 1152], P(('dp', 'seq'))
- weight_grad: float32 [1152, 1152], P('seq', 'dp')
The draws below stay inside these ranges and needn't reach their ends.
Inputs may be any that keep to these rules, and one draw needn't show every extreme that they name: `extents`: row i lists the 8 images packed in order into sequence i, in units of 64 tokens; each row sums to 16.
All inputs are finite; a program needn't handle non-finite values.
Results may differ from the reference program's by a relative error of at most 0.034.
Values may be sent and summed in bfloat16 or wider, within the bound.
A program may use at most 128 MiB of HBM per device.

```python
import math
import jax
import jax.numpy as jnp
import numpy as np
from jax import lax

D = 1152
HEADS = 16
HEAD = 72
IMAGES = 8
UNIT = 64
SEQ = 1024
TOKENS = 4096
SEQ_UNITS = 16
MOST_UNITS = 8
N_DP = 4


def draw_queries(key, part):
    key = jax.random.fold_in(key, 11)
    result = jnp.clip(jax.random.normal(key, (TOKENS, D), jnp.float32), -4.0, 4.0)
    return result.astype(jnp.bfloat16)


def draw_keys(key, part):
    key = jax.random.fold_in(key, 23)
    result = jnp.clip(jax.random.normal(key, (TOKENS, D), jnp.float32), -4.0, 4.0)
    return result.astype(jnp.bfloat16)


def strengthened(drawn, stream_key, source, target, parts, factor):
    def block_of(axis_at):
        return (jnp.arange(drawn.shape[axis_at]) // (drawn.shape[axis_at] // parts)).reshape((-1,) + (1,) * (drawn.ndim - 1 - axis_at))

    one_side = jax.random.permutation(stream_key, parts)[block_of(target)]
    other_side = (block_of(target) + parts // 2) % parts
    return jnp.where((block_of(source) == one_side) | (block_of(source) == other_side), factor * drawn, drawn)


def steps_of(stream_key, dims, pieces, smallest, top_value):
    def one(dim, parts):
        heights = jax.random.uniform(jax.random.fold_in(jax.random.fold_in(stream_key, 6), dim), (parts,), jnp.float32, smallest / len(pieces), top_value / len(pieces))
        return jnp.repeat(jnp.exp(heights), dims[dim] // parts).reshape((-1,) + (1,) * (len(dims) - dim - 1))

    loudness = one(*pieces[0])
    for cut in pieces[1:]:
        loudness = loudness * one(*cut)
    return loudness


def length_profile(count, total, most, lean):
    loads = [(1 << 20) // math.isqrt(grade ** lean) + 1 for grade in range(2, count + 1)]
    rest, counts = total - most - (count - 1), [1] * (count - 1)
    while rest > 0:
        movable = [i for i in range(count - 1) if counts[i] < most]
        mass, budget = sum([loads[i] for i in movable]), rest
        for i in movable:
            extra = min(most - counts[i], max(1, budget * loads[i] // mass), rest)
            counts[i] = counts[i] + extra
            rest = rest - extra
    return np.array([most] + counts)


def uneven_parts(own_key, amount, total, limit, slope):
    if amount == 2:
        one = jax.random.randint(own_key, (), max(1, total - limit), min(limit, total - 1) + 1)
        return jnp.stack([one, total - one])
    sizes = jnp.asarray(length_profile(amount, total, limit, slope), jnp.int32)
    couples = (amount - 1) // 2
    source_of, receiver = sizes[1:1 + 2 * couples:2], sizes[2:2 + 2 * couples:2]
    slack = jnp.minimum(source_of - 1, limit - receiver)
    passed = jax.random.randint(jax.random.fold_in(own_key, 1), (couples,), 0, 1 << 20) % (slack + 1)
    sizes = sizes.at[1:1 + 2 * couples:2].set(source_of - passed).at[2:2 + 2 * couples:2].set(receiver + passed)
    return sizes[jax.random.permutation(jax.random.fold_in(own_key, 2), amount)]


def scatter_about(rng, extent, scale, bound, pieces=(), kind=jnp.bfloat16):
    factor_of = steps_of(rng, extent, pieces, -0.22, 0.18) if pieces else 1.0
    drawn = jax.random.normal(rng, extent, jnp.float32) * scale * factor_of
    return jnp.minimum(jnp.maximum(drawn, -bound), bound).astype(kind)


def bell_draw_with(stream_key, extent, spread, reach, shards, heavy, kind=jnp.bfloat16):
    array = spread * jax.random.normal(stream_key, extent, jnp.float32)
    if shards:
        array = array * steps_of(stream_key, extent, shards, -0.22, 0.18)
    return jnp.clip(strengthened(array, jax.random.fold_in(stream_key, 3), *heavy), -reach, reach).astype(kind)


def setup_inputs(seed: int = 0) -> dict:
    key_of = jax.random.split(jax.random.key(seed), 7)
    queries = draw_queries(jax.random.fold_in(key_of[6], 71), 0)
    keys = draw_keys(jax.random.fold_in(key_of[6], 71), 0)
    values = scatter_about(key_of[2], (TOKENS, D), 1.0, 6.0, ((0, 32),))
    out_grad = bell_draw_with(key_of[3], (TOKENS, D), 1.0, 6.0, ((0, 32),), (0, 1, 32, 2.75))
    out_weight = scatter_about(key_of[4], (D, D), D ** -0.5, 0.1875)
    extents = jax.vmap(lambda own: uneven_parts(own, IMAGES, SEQ_UNITS, MOST_UNITS, 2))(jax.random.split(key_of[5], N_DP)).reshape((N_DP, IMAGES)).astype(jnp.int32)
    return dict(queries=queries, keys=keys, values=values, out_grad=out_grad, out_weight=out_weight, extents=extents)


def attend_head(query_head, key_head, value_head, back_head, same):
    score_scale = HEAD ** -0.5
    scores = jnp.dot(query_head, key_head.T, preferred_element_type=jnp.float32) * score_scale
    masked = jnp.where(same, scores, -1e30)
    top_score = jnp.max(masked, axis=1, keepdims=True)
    total = jnp.sum(jnp.where(same, jnp.exp(scores - top_score), 0.0), axis=1, keepdims=True)
    log_total = top_score + jnp.log(total)
    probs = jnp.where(same, jnp.exp(scores - log_total), 0.0)
    probs_low = probs.astype(jnp.bfloat16)
    attended = jnp.dot(probs_low, value_head, preferred_element_type=jnp.float32).astype(jnp.bfloat16)
    delta = jnp.sum(back_head.astype(jnp.float32) * attended.astype(jnp.float32), axis=1, keepdims=True)
    dprobs = jnp.dot(back_head, value_head.T, preferred_element_type=jnp.float32)
    dscores = (probs * (dprobs - delta)).astype(jnp.bfloat16)
    query_grad = (jnp.dot(dscores, key_head, preferred_element_type=jnp.float32) * score_scale).astype(jnp.bfloat16)
    key_grad = (jnp.dot(dscores.T, query_head, preferred_element_type=jnp.float32) * score_scale).astype(jnp.bfloat16)
    value_grad = jnp.dot(probs_low.T, back_head, preferred_element_type=jnp.float32).astype(jnp.bfloat16)
    return attended, query_grad, key_grad, value_grad


def split_heads(matrix):
    return matrix.reshape(SEQ, HEADS, HEAD).transpose(1, 0, 2)


def merge_heads(stacked):
    return stacked.transpose(1, 0, 2).reshape(SEQ, D)


def sequence_grads(inputs, out_weight):
    queries, keys, values, out_grad, extent_row = inputs
    image_ends = jnp.cumsum(extent_row).astype(jnp.int32) * UNIT
    position = jnp.arange(SEQ, dtype=jnp.int32)
    segment = jnp.sum((position[:, None] >= image_ends[None, :]).astype(jnp.int32), axis=1)
    same = segment[:, None] == segment[None, :]
    out_back = jnp.dot(out_grad, out_weight.T, preferred_element_type=jnp.float32).astype(jnp.bfloat16)

    def one_head(head_inputs):
        return attend_head(head_inputs[0], head_inputs[1], head_inputs[2], head_inputs[3], same)

    attended, query_grad, key_grad, value_grad = lax.map(
        one_head, (split_heads(queries), split_heads(keys), split_heads(values), split_heads(out_back)))
    return merge_heads(attended), merge_heads(query_grad), merge_heads(key_grad), merge_heads(value_grad)


def reference(queries, keys, values, out_grad, out_weight, extents):
    def per_sequence(inputs):
        return sequence_grads(inputs, out_weight)

    stacked = (queries.reshape(N_DP, SEQ, D), keys.reshape(N_DP, SEQ, D), values.reshape(N_DP, SEQ, D),
               out_grad.reshape(N_DP, SEQ, D), extents)
    attended, query_grad, key_grad, value_grad = lax.map(per_sequence, stacked)
    attended = attended.reshape(TOKENS, D)
    weight_grad = jnp.dot(attended.T, out_grad, preferred_element_type=jnp.float32)
    return (query_grad.reshape(TOKENS, D), key_grad.reshape(TOKENS, D), value_grad.reshape(TOKENS, D), weight_grad)
```

```python
import functools
import math

import jax
import jax.numpy as jnp
from jax import lax
from jax.experimental import pallas as pl
from jax.experimental.pallas import tpu as pltpu
from jax.sharding import PartitionSpec as P

HEADS = 16
HEAD = 72
UNIT = 64
BAND = 80
FAR = -float(2.0**60)
F32 = jnp.float32
BF16 = jnp.bfloat16
MESH = pl.DeviceIdType.MESH
NT = (((1,), (1,)), ((), ()))
NN = (((1,), (0,)), ((), ()))


def dot(a, b, dims=NN):
    return lax.dot_general(a, b, dims, preferred_element_type=F32)


def kernel(
    n, ndp, images, ext_ref, q_ref, k_ref, v_ref, og_ref, w_ref,
    dq_ref, dk_ref, dv_ref, dw_ref,
    og_all, w_mine, flip, send_a, send_b, recv_a, recv_b,
    ret_a, ret_b, back_a, back_b,
    xq, xk, xv, xd, kn, vn, do_t, att_t, dq_s, dk_s, dv_s, w_out, w_in,
    sem_sa, sem_ra, sem_sb, sem_rb, sem_ta, sem_ka, sem_tb, sem_kb,
    sem_og, sem_up, sem_down, sem_sib, sem_ws, sem_wr, sem_w,
):
    rows, width = q_ref.shape
    per = HEADS // n
    span = per * HEAD
    seq = n * rows
    two = per == 2
    low = 64 if two else BAND
    line = n // 2
    me = lax.axis_index("seq")
    dp = lax.axis_index("dp")
    z = me // 2
    core = lax.rem(me, 2)
    sib = me + 1 - 2 * core
    groups = width // rows

    if w_ref.shape[0] == span:
        w_copy = pltpu.make_async_copy(w_ref, w_mine, sem_w)
    else:
        at = pl.multiple_of(me * span, span)
        w_copy = pltpu.make_async_copy(w_ref.at[pl.ds(at, span), :], w_mine, sem_w)
    w_copy.start()

    barrier = pltpu.get_barrier_semaphore()
    for p in range(1, n):
        pl.semaphore_signal(
            barrier, inc=1, device_id={"seq": lax.rem(me + p, n)}, device_id_type=MESH
        )
    for p in range(1, ndp):
        pl.semaphore_signal(
            barrier, inc=1, device_id={"dp": lax.rem(dp + p, ndp)}, device_id_type=MESH
        )

    og_all[pl.ds(me, 1)] = og_ref[...][None]

    def pack(ref, which):
        for g in range(groups):
            part = ref[:, g * rows:(g + 1) * rows].astype(F32)
            flip[g * rows:(g + 1) * rows, :] = part.T
        for d in range(n):
            base = d * span
            if two:
                send_a[d, which * BAND:(which + 1) * BAND, :] = flip[base:base + BAND, :].astype(BF16)
                send_b[d, which * 64:(which + 1) * 64, :] = flip[base + BAND:base + span, :].astype(BF16)
            else:
                padded = jnp.concatenate(
                    [flip[base:base + span, :], jnp.zeros((BAND - span, rows), F32)], axis=0
                )
                send_a[d, which * BAND:(which + 1) * BAND, :] = padded.astype(BF16)

    pack(q_ref, 0)
    pack(k_ref, 1)
    pack(v_ref, 2)
    pl.semaphore_wait(barrier, n - 1 + ndp - 1)

    def relay(src, send_sem, target):
        return pltpu.make_async_remote_copy(
            src_ref=og_all.at[src],
            dst_ref=og_all.at[src],
            send_sem=send_sem,
            recv_sem=sem_og.at[src],
            device_id={"seq": target},
            device_id_type=MESH,
        )

    def exchange(out, into, send_sem, recv_sem, peer, slot):
        return pltpu.make_async_remote_copy(
            src_ref=out.at[peer],
            dst_ref=into.at[slot],
            send_sem=send_sem.at[peer],
            recv_sem=recv_sem.at[slot],
            device_id={"seq": peer},
            device_id_type=MESH,
        )

    def send_all(out, into, send_sem, recv_sem):
        @pl.loop(1, n)
        def _(p):
            exchange(out, into, send_sem, recv_sem, lax.rem(me + p, n), me).start()

    def wait_all(out, into, send_sem, recv_sem):
        @pl.loop(1, n)
        def _(p):
            peer = lax.rem(me + p, n)
            exchange(out, into, send_sem, recv_sem, peer, peer).wait_recv()

    def wait_sent(out, into, send_sem, recv_sem):
        @pl.loop(1, n)
        def _(p):
            peer = lax.rem(me + p, n)
            exchange(out, into, send_sem, recv_sem, peer, peer).wait_send()

    can_up = z < line - 1
    can_down = z > 0

    @pl.when(can_up)
    def _():
        relay(me, sem_up.at[z], me + 2).start()

    @pl.when(can_down)
    def _():
        relay(me, sem_down.at[z], me - 2).start()

    relay(me, sem_sib.at[z], sib).start()
    set_a = (send_a, recv_a, sem_sa, sem_ra)
    set_b = (send_b, recv_b, sem_sb, sem_rb)
    send_all(*set_a)
    recv_a[pl.ds(me, 1)] = send_a[pl.ds(me, 1)]
    if two:
        recv_b[pl.ds(me, 1)] = send_b[pl.ds(me, 1)]

    for step in range(1, line):
        @pl.when(z >= step)
        def _():
            src = me - 2 * step
            relay(src, sem_up.at[z - step], sib).wait_recv()

            @pl.when(can_up)
            def _():
                relay(src, sem_up.at[z - step], me + 2).start()

            relay(src, sem_sib.at[z - step], sib).start()

        @pl.when(z + step < line)
        def _():
            src = me + 2 * step
            relay(src, sem_down.at[z + step], sib).wait_recv()

            @pl.when(can_down)
            def _():
                relay(src, sem_down.at[z + step], me - 2).start()

            relay(src, sem_sib.at[z + step], sib).start()

        if step == 1 and two:
            send_all(*set_b)

    for other in range(line):
        relay(2 * other + 1 - core, sem_sib.at[other], sib).wait_recv()
    w_copy.wait()

    @pl.loop(0, n)
    def _(s):
        lanes = pl.ds(pl.multiple_of(s * rows, rows), rows)
        do_t[0:span, lanes] = dot(w_mine[...], og_all[s], NT)

    ends = []
    total = jnp.int32(0)
    for i in range(images):
        total = total + ext_ref[0, i] * UNIT
        ends.append(total)

    block = math.gcd(seq, 256)
    scale = HEAD ** (-0.5)
    turn = scale * math.log2(math.e)

    def head(h):
        first = 0 if h == 0 else 8
        feature = HEAD if h == 0 else 0
        off = 64 * h
        row = lax.broadcasted_iota(jnp.int32, (BAND, rows), 0)
        own = (row >= first) & (row < first + HEAD)
        for s in range(n):
            spot = lax.broadcasted_iota(jnp.int32, (BAND, rows), 1) + s * rows
            segment = jnp.zeros((BAND, rows), jnp.int32)
            for end in ends:
                segment = segment + (spot >= end).astype(jnp.int32)
            hit = (row - feature) == segment
            lanes = slice(s * rows, (s + 1) * rows)

            def take(which):
                if h == 0:
                    return recv_a[s, which * BAND:(which + 1) * BAND, :].astype(F32)
                return jnp.concatenate(
                    [
                        recv_a[s, which * BAND + 64:(which + 1) * BAND, :].astype(F32),
                        recv_b[s, which * 64:(which + 1) * 64, :].astype(F32),
                    ],
                    axis=0,
                )

            qs = jnp.where(own, take(0), jnp.where(hit, 1.0, 0.0))
            ks = jnp.where(own, take(1), jnp.where(hit, 0.0, FAR))
            vs = jnp.where(own, take(2), 0.0)
            xq[:, lanes] = qs.astype(BF16)
            xk[:, lanes] = ks.astype(BF16)
            xv[:, lanes] = vs.astype(BF16)
            kn[lanes, :] = ks.T.astype(BF16)
            vn[lanes, :] = vs.T.astype(BF16)
            xd[:, lanes] = jnp.where(own, do_t[off:off + BAND, lanes], 0.0).astype(BF16)

        dk_s[...] = jnp.zeros_like(dk_s)
        dv_s[...] = jnp.zeros_like(dv_s)

        @pl.loop(0, seq // block)
        def _(b):
            lanes = pl.ds(pl.multiple_of(b * block, block), block)
            q = xq[:, lanes]
            back = xd[:, lanes]
            scores = dot(kn[...], q)
            top = jnp.max(scores, axis=0, keepdims=True)
            grown = jnp.exp2((scores - top) * turn)
            inverse = 1.0 / jnp.sum(grown, axis=0, keepdims=True)
            probs = grown * inverse
            probs_low = probs.astype(BF16)
            attended = dot(xv[...], probs_low).astype(BF16).astype(F32)
            delta = jnp.sum(back.astype(F32) * attended, axis=0, keepdims=True)
            dprobs = dot(vn[...], back)
            dscores = (probs * (dprobs - delta)).astype(BF16)
            dq_s[:, lanes] = dot(xk[...], dscores) * scale
            dk_s[...] += dot(q, dscores, NT)
            dv_s[...] += dot(back, probs_low, NT)
            if h == 0:
                att_t[0:BAND, lanes] = attended
            else:
                att_t[72:80, lanes] = attended[8:16]
                att_t[80:144, lanes] = attended[16:80]

        for s in range(n):
            lanes = slice(s * rows, (s + 1) * rows)
            for which, ref in enumerate((dq_s, dk_s, dv_s)):
                part = ref[:, lanes]
                if which == 1:
                    part = part * scale
                if h == 0:
                    ret_a[s, which * low:(which + 1) * low, :] = part[0:low].astype(BF16)
                    if two:
                        ret_b[s, which * BAND:which * BAND + 16, :] = part[64:80].astype(BF16)
                else:
                    old = ret_b[s, which * BAND:which * BAND + 16, :].astype(F32)
                    part = jnp.concatenate([old[0:8], part[8:80]], axis=0)
                    ret_b[s, which * BAND:(which + 1) * BAND, :] = part.astype(BF16)

    wait_all(*set_a)
    head(0)
    set_ra = (ret_a, back_a, sem_ta, sem_ka)
    set_rb = (ret_b, back_b, sem_tb, sem_kb)
    send_all(*set_ra)
    back_a[pl.ds(me, 1)] = ret_a[pl.ds(me, 1)]
    if two:
        wait_all(*set_b)
        head(1)
        send_all(*set_rb)
        back_b[pl.ds(me, 1)] = ret_b[pl.ds(me, 1)]

    piece = width // ndp
    term = jnp.zeros((span, width), F32)
    term = dot(att_t[0:span, :].astype(BF16), og_all[...].reshape(seq, width))
    for j in range(ndp):
        w_out[j, 0:span, :] = term[:, j * piece:(j + 1) * piece].astype(BF16)

    def reduce_copy(peer, slot):
        return pltpu.make_async_remote_copy(
            src_ref=w_out.at[peer],
            dst_ref=w_in.at[slot],
            send_sem=sem_ws.at[peer],
            recv_sem=sem_wr.at[slot],
            device_id={"dp": peer},
            device_id_type=MESH,
        )

    for p in range(1, ndp):
        reduce_copy(lax.rem(dp + p, ndp), dp).start()
    w_in[pl.ds(dp, 1)] = w_out[pl.ds(dp, 1)]
    for p in range(1, ndp):
        peer = lax.rem(dp + p, ndp)
        reduce_copy(peer, peer).wait_recv()
    result = w_in[0, 0:span, :].astype(F32)
    for j in range(1, ndp):
        result = result + w_in[j, 0:span, :].astype(F32)
    dw_ref[...] = result

    wait_all(*set_ra)
    if two:
        wait_all(*set_rb)
    for which, out in enumerate((dq_ref, dk_ref, dv_ref)):
        for d in range(n):
            base = d * span
            first = back_a[d, which * low:(which + 1) * low, :].astype(F32)
            if two:
                flip[base:base + 64, :] = first
                flip[base + 64:base + span, :] = back_b[
                    d, which * BAND:(which + 1) * BAND, :
                ].astype(F32)
            else:
                flip[base:base + span, :] = first[0:span]
        for g in range(groups):
            out[:, g * rows:(g + 1) * rows] = flip[g * rows:(g + 1) * rows, :].T.astype(BF16)

    wait_sent(*set_a)
    wait_sent(*set_ra)
    if two:
        wait_sent(*set_b)
        wait_sent(*set_rb)
    for p in range(1, ndp):
        peer = lax.rem(dp + p, ndp)
        reduce_copy(peer, peer).wait_send()
    for part in range(line):
        relay(2 * part + core, sem_sib.at[part], sib).wait_send()

        @pl.when(can_up & (z >= part))
        def _():
            relay(2 * part + core, sem_up.at[part], sib).wait_send()

        @pl.when(can_down & (z <= part))
        def _():
            relay(2 * part + core, sem_down.at[part], sib).wait_send()


def local(n, ndp, queries, keys, values, out_grad, out_weight, extents):
    rows, width = queries.shape
    per = HEADS // n
    assert per in (1, 2) and rows % 128 == 0
    span = per * HEAD
    padded = -(-span // 16) * 16
    seq = n * rows
    line = n // 2
    images = extents.shape[1]
    low = 64 if per == 2 else BAND
    if span % 16:
        out_weight = lax.dynamic_slice_in_dim(
            out_weight, lax.axis_index("seq") * span, span, axis=0
        )
    vmem = pl.BlockSpec(memory_space=pltpu.VMEM)
    grad = jax.ShapeDtypeStruct((rows, width), BF16)
    dma = pltpu.SemaphoreType.DMA
    buf = pltpu.VMEM
    return pl.pallas_call(
        functools.partial(kernel, n, ndp, images),
        out_shape=(grad, grad, grad, jax.ShapeDtypeStruct((span, width // ndp), F32)),
        in_specs=[
            pl.BlockSpec(memory_space=pltpu.SMEM), vmem, vmem, vmem, vmem,
            pl.BlockSpec(memory_space=pl.ANY),
        ],
        out_specs=(vmem, vmem, vmem, vmem),
        scratch_shapes=[
            buf((n, rows, width), BF16),
            buf((span, width), BF16),
            buf((width, rows), F32),
            buf((n, 3 * BAND, rows), BF16),
            buf((n, 3 * 64, rows), BF16),
            buf((n, 3 * BAND, rows), BF16),
            buf((n, 3 * 64, rows), BF16),
            buf((n, 3 * low, rows), BF16),
            buf((n, 3 * BAND, rows), BF16),
            buf((n, 3 * low, rows), BF16),
            buf((n, 3 * BAND, rows), BF16),
            buf((BAND, seq), BF16),
            buf((BAND, seq), BF16),
            buf((BAND, seq), BF16),
            buf((BAND, seq), BF16),
            buf((seq, BAND), BF16),
            buf((seq, BAND), BF16),
            buf((padded, seq), F32),
            buf((padded, seq), F32),
            buf((BAND, seq), F32),
            buf((BAND, seq), F32),
            buf((BAND, seq), F32),
            buf((ndp, padded, width // ndp), BF16),
            buf((ndp, padded, width // ndp), BF16),
        ]
        + [dma((n,))] * 8
        + [dma((n,)), dma((line,)), dma((line,)), dma((line,)), dma((ndp,)), dma((ndp,)), dma],
        compiler_params=pltpu.CompilerParams(
            collective_id=0, has_side_effects=True, vmem_limit_bytes=48 * 2**20
        ),
        cost_estimate=pl.CostEstimate(
            flops=10 * per * seq * seq * HEAD, bytes_accessed=10 * rows * width * 2,
            transcendentals=per * seq * seq,
        ),
    )(extents, queries, keys, values, out_grad, out_weight)


def solution(mesh):
    n, ndp = mesh.shape["seq"], mesh.shape["dp"]
    return jax.shard_map(
        functools.partial(local, n, ndp),
        mesh=mesh,
        in_specs=(
            P(("dp", "seq"), None),
            P(("dp", "seq"), None),
            P(("dp", "seq"), None),
            P(("dp", "seq"), None),
            P(),
            P("dp", None),
        ),
        out_specs=(
            P(("dp", "seq"), None),
            P(("dp", "seq"), None),
            P(("dp", "seq"), None),
            P("seq", "dp"),
        ),
        check_vma=False,
    )
```

```python
import functools
import math

import jax
import jax.numpy as jnp
from jax import lax
from jax.experimental import pallas as pl
from jax.experimental.pallas import tpu as pltpu
from jax.sharding import PartitionSpec as P

HEADS = 16
HEAD = 72
UNIT = 64
BAND = 80
FAR = -float(2.0**60)
F32 = jnp.float32
BF16 = jnp.bfloat16
MESH = pl.DeviceIdType.MESH
NT = (((1,), (1,)), ((), ()))
NN = (((1,), (0,)), ((), ()))


def dot(a, b, dims=NN):
    return lax.dot_general(a, b, dims, preferred_element_type=F32)


def kernel(
    n, ndp, images, ext_ref, q_hbm, k_hbm, v_hbm, og_hbm, w_ref,
    dq_ref, dk_ref, dv_ref, dw_ref,
    q_ref, k_ref, v_ref, og_all, w_mine, flip, send_a, send_b, recv_a, recv_b,
    ret_q, ret_kv, back_q, back_kv,
    xq, xk, xv, kn, vn, probs_all, att_t, dk_s, dv_s, w_out, w_in,
    sem_sa, sem_ra, sem_sb, sem_rb, sem_tq, sem_kq, sem_tk, sem_kk,
    sem_og, sem_up, sem_down, sem_sib, sem_ws, sem_wr, sem_in,
):
    rows, width = q_ref.shape
    per = HEADS // n
    span = per * HEAD
    seq = n * rows
    two = per == 2
    line = n // 2
    pair = 2 * rows
    me = lax.axis_index("seq")
    dp = lax.axis_index("dp")
    z = me // 2
    core = lax.rem(me, 2)
    sib = me + 1 - 2 * core
    groups = width // rows

    if w_ref.shape[0] == span:
        w_from = w_ref
    else:
        w_from = w_ref.at[pl.ds(pl.multiple_of(me * span, span), span), :]
    loads = [
        pltpu.make_async_copy(src, dst, sem_in.at[i])
        for i, (src, dst) in enumerate(
            [(og_hbm, og_all.at[me]), (q_hbm, q_ref), (k_hbm, k_ref), (v_hbm, v_ref), (w_from, w_mine)]
        )
    ]
    for load in loads:
        load.start()

    barrier = pltpu.get_barrier_semaphore()
    for p in range(1, n):
        pl.semaphore_signal(
            barrier, inc=1, device_id={"seq": lax.rem(me + p, n)}, device_id_type=MESH
        )
    for p in range(1, ndp):
        pl.semaphore_signal(
            barrier, inc=1, device_id={"dp": lax.rem(dp + p, ndp)}, device_id_type=MESH
        )

    def relay(src, send_sem, target):
        return pltpu.make_async_remote_copy(
            src_ref=og_all.at[src],
            dst_ref=og_all.at[src],
            send_sem=send_sem,
            recv_sem=sem_og.at[src],
            device_id={"seq": target},
            device_id_type=MESH,
        )

    def exchange(out, into, send_sem, recv_sem, peer, slot):
        return pltpu.make_async_remote_copy(
            src_ref=out.at[peer],
            dst_ref=into.at[slot],
            send_sem=send_sem.at[peer],
            recv_sem=recv_sem.at[slot],
            device_id={"seq": peer},
            device_id_type=MESH,
        )

    def send_all(out, into, send_sem, recv_sem):
        @pl.loop(1, n)
        def _(p):
            exchange(out, into, send_sem, recv_sem, lax.rem(me + p, n), me).start()

    def wait_all(out, into, send_sem, recv_sem):
        @pl.loop(1, n)
        def _(p):
            peer = lax.rem(me + p, n)
            exchange(out, into, send_sem, recv_sem, peer, peer).wait_recv()

    def wait_sent(out, into, send_sem, recv_sem):
        @pl.loop(1, n)
        def _(p):
            peer = lax.rem(me + p, n)
            exchange(out, into, send_sem, recv_sem, peer, peer).wait_send()

    set_a = (send_a, recv_a, sem_sa, sem_ra)
    set_b = (send_b, recv_b, sem_sb, sem_rb)
    set_q = (ret_q, back_q, sem_tq, sem_kq)
    set_kv = (ret_kv, back_kv, sem_tk, sem_kk)
    can_up = z < line - 1
    can_down = z > 0

    loads[1].wait()
    loads[2].wait()
    loads[3].wait()
    for which, ref in enumerate((q_ref, k_ref, v_ref)):
        for g in range(groups):
            part = ref[:, g * rows:(g + 1) * rows].astype(F32)
            flip[which, g * rows:(g + 1) * rows, :] = part.T
        for d in range(n):
            base = d * span
            if two:
                part = flip[which, base:base + BAND, :]
            else:
                part = jnp.concatenate(
                    [flip[which, base:base + span, :], jnp.zeros((BAND - span, rows), F32)], axis=0
                )
            send_a[d, which * BAND:(which + 1) * BAND, :] = part.astype(BF16)
    loads[0].wait()
    pl.semaphore_wait(barrier, n - 1 + ndp - 1)
    send_all(*set_a)

    @pl.when(can_up)
    def _():
        relay(me, sem_up.at[z], me + 2).start()

    @pl.when(can_down)
    def _():
        relay(me, sem_down.at[z], me - 2).start()

    relay(me, sem_sib.at[z], sib).start()
    recv_a[pl.ds(me, 1)] = send_a[pl.ds(me, 1)]
    if two:
        for which in range(3):
            for d in range(n):
                base = d * span
                send_b[d, which * 64:(which + 1) * 64, :] = flip[
                    which, base + BAND:base + span, :
                ].astype(BF16)
        send_all(*set_b)
        recv_b[pl.ds(me, 1)] = send_b[pl.ds(me, 1)]

    def relay_step(step):
        @pl.when(z >= step)
        def _():
            src = me - 2 * step
            relay(src, sem_up.at[z - step], sib).wait_recv()

            @pl.when(can_up)
            def _():
                relay(src, sem_up.at[z - step], me + 2).start()

            relay(src, sem_sib.at[z - step], sib).start()

        @pl.when(z + step < line)
        def _():
            src = me + 2 * step
            relay(src, sem_down.at[z + step], sib).wait_recv()

            @pl.when(can_down)
            def _():
                relay(src, sem_down.at[z + step], me - 2).start()

            relay(src, sem_sib.at[z + step], sib).start()

    ends = []
    total = jnp.int32(0)
    for i in range(images):
        total = total + ext_ref[0, i] * UNIT
        ends.append(total)

    scale = HEAD ** (-0.5)
    turn = scale * math.log2(math.e)

    def owned(h, lanes):
        row = lax.broadcasted_iota(jnp.int32, (BAND, lanes), 0)
        first = 0 if h == 0 else 8
        return (row >= first) & (row < first + HEAD)

    def forward(h):
        feature = HEAD if h == 0 else 0
        row = lax.broadcasted_iota(jnp.int32, (BAND, rows), 0)
        own = owned(h, rows)
        for s in range(n):
            spot = lax.broadcasted_iota(jnp.int32, (1, rows), 1) + s * rows
            segment = jnp.zeros((1, rows), jnp.int32)
            for end in ends:
                segment = segment + (spot >= end).astype(jnp.int32)
            hit = (row - feature) == segment
            lanes = slice(s * rows, (s + 1) * rows)

            def take(which):
                if h == 0:
                    return recv_a[s, which * BAND:(which + 1) * BAND, :].astype(F32)
                return jnp.concatenate(
                    [
                        recv_a[s, which * BAND + 64:(which + 1) * BAND, :].astype(F32),
                        recv_b[s, which * 64:(which + 1) * 64, :].astype(F32),
                    ],
                    axis=0,
                )

            qs = jnp.where(own, take(0), jnp.where(hit, 1.0, 0.0))
            ks = jnp.where(own, take(1), jnp.where(hit, 0.0, FAR))
            vs = jnp.where(own, take(2), 0.0)
            xq[h, :, lanes] = qs.astype(BF16)
            xk[h, :, lanes] = ks.astype(BF16)
            xv[h, :, lanes] = vs.astype(BF16)
            kn[h, lanes, :] = ks.T.astype(BF16)
            vn[h, lanes, :] = vs.T.astype(BF16)

        dk_s[h] = jnp.zeros((BAND, seq), F32)
        dv_s[h] = jnp.zeros((BAND, seq), F32)

        @pl.loop(0, line)
        def _(b):
            lanes = pl.ds(pl.multiple_of(b * pair, pair), pair)
            scores = dot(kn[h], xq[h, :, lanes])
            top = jnp.max(scores, axis=0, keepdims=True)
            grown = jnp.exp2((scores - top) * turn)
            inverse = 1.0 / jnp.sum(grown, axis=0, keepdims=True)
            probs = grown * inverse
            probs_all[h, :, lanes] = probs
            attended = dot(xv[h], probs.astype(BF16)).astype(BF16).astype(F32)
            if h == 0:
                att_t[0:BAND, lanes] = attended
            else:
                att_t[72:80, lanes] = attended[8:16]
                att_t[80:144, lanes] = attended[16:80]

    def backward(chip):
        lanes = pl.ds(pl.multiple_of(chip * pair, pair), pair)
        held = og_all[pl.ds(2 * chip, 2)].reshape(pair, width)
        backs = dot(w_mine[...], held, NT)
        if not two:
            backs = jnp.concatenate([backs, jnp.zeros((BAND - span, pair), F32)], axis=0)
        parts = []
        for h in range(per):
            off = 64 * h
            back = jnp.where(owned(h, pair), backs[off:off + BAND], 0.0).astype(BF16)
            delta = jnp.sum(
                back.astype(F32) * att_t[off:off + BAND, lanes], axis=0, keepdims=True
            )
            probs = probs_all[h, :, lanes]
            dprobs = dot(vn[h], back)
            dscores = (probs * (dprobs - delta)).astype(BF16)
            parts.append(dot(xk[h], dscores) * scale)
            dk_s[h] += dot(xq[h, :, lanes], dscores, NT)
            dv_s[h] += dot(back, probs.astype(BF16), NT)
        done = jnp.concatenate([parts[0][0:72], parts[1][8:80]], axis=0) if two else parts[0]
        for j in range(2):
            peer = 2 * chip + j
            block = done[:, j * rows:(j + 1) * rows].astype(BF16)
            ret_q[pl.ds(peer, 1)] = block[None]

            @pl.when(peer != me)
            def _():
                exchange(*set_q, peer, me).start()

    wait_all(*set_a)
    forward(0)
    relay_step(1)
    if two:
        wait_all(*set_b)
        forward(1)
    if line > 2:
        relay_step(2)
    loads[4].wait()
    near = jnp.minimum(z, line - 1 - z)
    toward = jnp.where(z < line - 1 - z, 1, -1)

    @pl.loop(0, line)
    def _(i):
        @pl.when((i >= 2) & (i + 1 < line))
        def _():
            relay_step(i + 1)

        swing = ((i + 1) // 2) * (1 - 2 * lax.rem(i, 2))
        chip = z + jnp.where(i <= 2 * near, swing, toward * (i - near))
        relay(2 * chip + 1 - core, sem_sib.at[chip], sib).wait_recv()
        backward(chip)

    tall = ret_q.shape[1]
    for s in range(n):
        lanes = slice(s * rows, (s + 1) * rows)
        for which, (ref, factor) in enumerate(((dk_s, scale), (dv_s, None))):
            if two:
                part = jnp.concatenate([ref[0, 0:72, lanes], ref[1, 8:80, lanes]], axis=0)
            else:
                part = ref[0, :, lanes]
            if factor is not None:
                part = part * factor
            ret_kv[s, which * tall:(which + 1) * tall, :] = part.astype(BF16)
    send_all(*set_kv)
    back_q[pl.ds(me, 1)] = ret_q[pl.ds(me, 1)]
    back_kv[pl.ds(me, 1)] = ret_kv[pl.ds(me, 1)]

    piece = width // ndp
    term = dot(att_t[0:span, :].astype(BF16), og_all[...].reshape(seq, width))
    for j in range(ndp):
        w_out[j, 0:span, :] = term[:, j * piece:(j + 1) * piece].astype(BF16)

    def reduce_copy(peer, slot):
        return pltpu.make_async_remote_copy(
            src_ref=w_out.at[peer],
            dst_ref=w_in.at[slot],
            send_sem=sem_ws.at[peer],
            recv_sem=sem_wr.at[slot],
            device_id={"dp": peer},
            device_id_type=MESH,
        )

    for p in range(1, ndp):
        reduce_copy(lax.rem(dp + p, ndp), dp).start()
    w_in[pl.ds(dp, 1)] = w_out[pl.ds(dp, 1)]

    def unpack(ref, first, out):
        for d in range(n):
            flip[0, d * span:(d + 1) * span, :] = ref[d, first:first + tall, :].astype(F32)[0:span]
        for g in range(groups):
            out[:, g * rows:(g + 1) * rows] = flip[0, g * rows:(g + 1) * rows, :].T.astype(BF16)

    wait_all(*set_q)
    unpack(back_q, 0, dq_ref)
    for p in range(1, ndp):
        peer = lax.rem(dp + p, ndp)
        reduce_copy(peer, peer).wait_recv()
    result = w_in[0, 0:span, :].astype(F32)
    for j in range(1, ndp):
        result = result + w_in[j, 0:span, :].astype(F32)
    dw_ref[...] = result
    wait_sent(*set_a)
    wait_sent(*set_q)
    if two:
        wait_sent(*set_b)
    for p in range(1, ndp):
        peer = lax.rem(dp + p, ndp)
        reduce_copy(peer, peer).wait_send()
    for part in range(line):
        relay(2 * part + core, sem_sib.at[part], sib).wait_send()

        @pl.when(can_up & (z >= part))
        def _():
            relay(2 * part + core, sem_up.at[part], sib).wait_send()

        @pl.when(can_down & (z <= part))
        def _():
            relay(2 * part + core, sem_down.at[part], sib).wait_send()

    wait_all(*set_kv)
    unpack(back_kv, 0, dk_ref)
    unpack(back_kv, tall, dv_ref)
    wait_sent(*set_kv)


def finish(*refs):
    count = len(refs) // 2
    sems = refs[-1]
    copies = [
        pltpu.make_async_copy(refs[i], refs[count + i], sems.at[i]) for i in range(count)
    ]
    for copy in copies:
        copy.start()
    for copy in copies:
        copy.wait()


def local(n, ndp, queries, keys, values, out_grad, out_weight, extents):
    rows, width = queries.shape
    per = HEADS // n
    assert per in (1, 2) and rows % 128 == 0
    span = per * HEAD
    padded = -(-span // 16) * 16
    seq = n * rows
    line = n // 2
    images = extents.shape[1]
    if span % 16:
        out_weight = lax.dynamic_slice_in_dim(
            out_weight, lax.axis_index("seq") * span, span, axis=0
        )
    vmem = pl.BlockSpec(memory_space=pltpu.VMEM)
    hbm = pl.BlockSpec(memory_space=pl.ANY)
    grad = jax.ShapeDtypeStruct((rows, width), BF16)
    weight = jax.ShapeDtypeStruct((span, width // ndp), F32)
    dma = pltpu.SemaphoreType.DMA
    buf = pltpu.VMEM
    parts = pl.pallas_call(
        functools.partial(kernel, n, ndp, images),
        out_shape=(grad, grad, grad, weight),
        in_specs=[pl.BlockSpec(memory_space=pltpu.SMEM), hbm, hbm, hbm, hbm, hbm],
        out_specs=(vmem, vmem, vmem, vmem),
        scratch_shapes=[
            buf((rows, width), BF16),
            buf((rows, width), BF16),
            buf((rows, width), BF16),
            buf((n, rows, width), BF16),
            buf((span, width), BF16),
            buf((3, width, rows), F32),
            buf((n, 3 * BAND, rows), BF16),
            buf((n, 3 * 64, rows), BF16),
            buf((n, 3 * BAND, rows), BF16),
            buf((n, 3 * 64, rows), BF16),
            buf((n, padded, rows), BF16),
            buf((n, 2 * padded, rows), BF16),
            buf((n, padded, rows), BF16),
            buf((n, 2 * padded, rows), BF16),
            buf((per, BAND, seq), BF16),
            buf((per, BAND, seq), BF16),
            buf((per, BAND, seq), BF16),
            buf((per, seq, BAND), BF16),
            buf((per, seq, BAND), BF16),
            buf((per, seq, seq), F32),
            buf((padded, seq), F32),
            buf((per, BAND, seq), F32),
            buf((per, BAND, seq), F32),
            buf((ndp, padded, width // ndp), BF16),
            buf((ndp, padded, width // ndp), BF16),
        ]
        + [dma((n,))] * 8
        + [dma((n,)), dma((line,)), dma((line,)), dma((line,)), dma((ndp,)), dma((ndp,)), dma((5,))],
        compiler_params=pltpu.CompilerParams(
            collective_id=0, has_side_effects=True, vmem_limit_bytes=56 * 2**20
        ),
        cost_estimate=pl.CostEstimate(
            flops=10 * per * seq * seq * HEAD, bytes_accessed=10 * rows * width * 2,
            transcendentals=per * seq * seq,
        ),
    )(extents, queries, keys, values, out_grad, out_weight)
    return pl.pallas_call(
        finish,
        out_shape=(grad, grad, grad, weight),
        in_specs=[hbm] * 4,
        out_specs=(hbm, hbm, hbm, hbm),
        scratch_shapes=[dma((4,))],
        compiler_params=pltpu.CompilerParams(vmem_limit_bytes=56 * 2**20),
    )(*parts)


def solution(mesh):
    n, ndp = mesh.shape["seq"], mesh.shape["dp"]
    return jax.shard_map(
        functools.partial(local, n, ndp),
        mesh=mesh,
        in_specs=(
            P(("dp", "seq"), None),
            P(("dp", "seq"), None),
            P(("dp", "seq"), None),
            P(("dp", "seq"), None),
            P(),
            P("dp", None),
        ),
        out_specs=(
            P(("dp", "seq"), None),
            P(("dp", "seq"), None),
            P(("dp", "seq"), None),
            P("seq", "dp"),
        ),
        check_vma=False,
    )
```

```python
import functools
import math

import jax
import jax.numpy as jnp
from jax import lax
from jax.experimental import pallas as pl
from jax.experimental.pallas import tpu as pltpu
from jax.sharding import PartitionSpec as P

HEADS = 16
HEAD = 72
UNIT = 64
BAND = 80
FAR = -float(2.0**60)
F32 = jnp.float32
BF16 = jnp.bfloat16
MESH = pl.DeviceIdType.MESH
NT = (((1,), (1,)), ((), ()))
NN = (((1,), (0,)), ((), ()))


def dot(a, b, dims=NN):
    return lax.dot_general(a, b, dims, preferred_element_type=F32)


def kernel(
    n, ndp, images, ext_ref, q_hbm, k_hbm, v_hbm, og_hbm, w_ref,
    dq_ref, dk_ref, dv_ref, dw_ref,
    q_ref, k_ref, v_ref, og_all, w_mine, flip, send_a, send_b, recv_a, recv_b,
    ret_q, ret_k, ret_v, back_q, back_k, back_v,
    xq, xk, xv, kn, vn, probs_all, att_t, dk_s, dv_s, w_out, w_in,
    sem_sa, sem_ra, sem_sb, sem_rb, sem_tq, sem_kq, sem_tk, sem_kk, sem_tv, sem_kv,
    sem_og, sem_up, sem_down, sem_sib, sem_ws, sem_wr, sem_in,
):
    rows, width = q_ref.shape
    per = HEADS // n
    span = per * HEAD
    seq = n * rows
    two = per == 2
    line = n // 2
    pair = 2 * rows
    me = lax.axis_index("seq")
    dp = lax.axis_index("dp")
    z = me // 2
    core = lax.rem(me, 2)
    sib = me + 1 - 2 * core
    groups = width // rows

    if w_ref.shape[0] == span:
        w_from = w_ref
    else:
        w_from = w_ref.at[pl.ds(pl.multiple_of(me * span, span), span), :]
    loads = [
        pltpu.make_async_copy(src, dst, sem_in.at[i])
        for i, (src, dst) in enumerate(
            [(og_hbm, og_all.at[me]), (q_hbm, q_ref), (k_hbm, k_ref), (v_hbm, v_ref), (w_from, w_mine)]
        )
    ]
    for load in loads:
        load.start()

    barrier = pltpu.get_barrier_semaphore()
    for p in range(1, n):
        pl.semaphore_signal(
            barrier, inc=1, device_id={"seq": lax.rem(me + p, n)}, device_id_type=MESH
        )
    for p in range(1, ndp):
        pl.semaphore_signal(
            barrier, inc=1, device_id={"dp": lax.rem(dp + p, ndp)}, device_id_type=MESH
        )

    def relay(src, send_sem, target):
        return pltpu.make_async_remote_copy(
            src_ref=og_all.at[src],
            dst_ref=og_all.at[src],
            send_sem=send_sem,
            recv_sem=sem_og.at[src],
            device_id={"seq": target},
            device_id_type=MESH,
        )

    def exchange(out, into, send_sem, recv_sem, peer, slot):
        return pltpu.make_async_remote_copy(
            src_ref=out.at[peer],
            dst_ref=into.at[slot],
            send_sem=send_sem.at[peer],
            recv_sem=recv_sem.at[slot],
            device_id={"seq": peer},
            device_id_type=MESH,
        )

    def send_all(out, into, send_sem, recv_sem):
        @pl.loop(1, n)
        def _(p):
            exchange(out, into, send_sem, recv_sem, lax.rem(me + p, n), me).start()

    def wait_all(out, into, send_sem, recv_sem):
        @pl.loop(1, n)
        def _(p):
            peer = lax.rem(me + p, n)
            exchange(out, into, send_sem, recv_sem, peer, peer).wait_recv()

    def wait_sent(out, into, send_sem, recv_sem):
        @pl.loop(1, n)
        def _(p):
            peer = lax.rem(me + p, n)
            exchange(out, into, send_sem, recv_sem, peer, peer).wait_send()

    set_a = (send_a, recv_a, sem_sa, sem_ra)
    set_b = (send_b, recv_b, sem_sb, sem_rb)
    set_q = (ret_q, back_q, sem_tq, sem_kq)
    set_k = (ret_k, back_k, sem_tk, sem_kk)
    set_v = (ret_v, back_v, sem_tv, sem_kv)
    can_up = z < line - 1
    can_down = z > 0

    loads[0].wait()
    pl.semaphore_wait(barrier, n - 1 + ndp - 1)

    @pl.when(can_up)
    def _():
        relay(me, sem_up.at[z], me + 2).start()

    @pl.when(can_down)
    def _():
        relay(me, sem_down.at[z], me - 2).start()

    relay(me, sem_sib.at[z], sib).start()

    loads[1].wait()
    loads[2].wait()
    loads[3].wait()
    for which, ref in enumerate((q_ref, k_ref, v_ref)):
        for g in range(groups):
            part = ref[:, g * rows:(g + 1) * rows].astype(F32)
            flip[which, g * rows:(g + 1) * rows, :] = part.T
        for d in range(n):
            base = d * span
            if two:
                part = flip[which, base:base + BAND, :]
            else:
                part = jnp.concatenate(
                    [flip[which, base:base + span, :], jnp.zeros((BAND - span, rows), F32)], axis=0
                )
            send_a[d, which * BAND:(which + 1) * BAND, :] = part.astype(BF16)
    send_all(*set_a)
    recv_a[pl.ds(me, 1)] = send_a[pl.ds(me, 1)]
    def relay_step(step):
        @pl.when(z >= step)
        def _():
            src = me - 2 * step
            relay(src, sem_up.at[z - step], sib).wait_recv()

            @pl.when(can_up)
            def _():
                relay(src, sem_up.at[z - step], me + 2).start()

            relay(src, sem_sib.at[z - step], sib).start()

        @pl.when(z + step < line)
        def _():
            src = me + 2 * step
            relay(src, sem_down.at[z + step], sib).wait_recv()

            @pl.when(can_down)
            def _():
                relay(src, sem_down.at[z + step], me - 2).start()

            relay(src, sem_sib.at[z + step], sib).start()

    if two:
        for which in range(3):
            for d in range(n):
                base = d * span
                send_b[d, which * 64:(which + 1) * 64, :] = flip[
                    which, base + BAND:base + span, :
                ].astype(BF16)
        relay_step(1)
        send_all(*set_b)
        recv_b[pl.ds(me, 1)] = send_b[pl.ds(me, 1)]

    ends = []
    total = jnp.int32(0)
    for i in range(images):
        total = total + ext_ref[0, i] * UNIT
        ends.append(total)

    scale = HEAD ** (-0.5)
    turn = scale * math.log2(math.e)

    def owned(h, lanes):
        row = lax.broadcasted_iota(jnp.int32, (BAND, lanes), 0)
        first = 0 if h == 0 else 8
        return (row >= first) & (row < first + HEAD)

    def forward(h):
        feature = HEAD if h == 0 else 0
        row = lax.broadcasted_iota(jnp.int32, (BAND, rows), 0)
        own = owned(h, rows)
        for s in range(n):
            spot = lax.broadcasted_iota(jnp.int32, (1, rows), 1) + s * rows
            segment = jnp.zeros((1, rows), jnp.int32)
            for end in ends:
                segment = segment + (spot >= end).astype(jnp.int32)
            hit = (row - feature) == segment
            lanes = slice(s * rows, (s + 1) * rows)

            def take(which):
                if h == 0:
                    return recv_a[s, which * BAND:(which + 1) * BAND, :].astype(F32)
                return jnp.concatenate(
                    [
                        recv_a[s, which * BAND + 64:(which + 1) * BAND, :].astype(F32),
                        recv_b[s, which * 64:(which + 1) * 64, :].astype(F32),
                    ],
                    axis=0,
                )

            qs = jnp.where(own, take(0), jnp.where(hit, 1.0, 0.0))
            ks = jnp.where(own, take(1), jnp.where(hit, 0.0, FAR))
            vs = jnp.where(own, take(2), 0.0)
            xq[h, :, lanes] = qs.astype(BF16)
            xk[h, :, lanes] = ks.astype(BF16)
            xv[h, :, lanes] = vs.astype(BF16)
            kn[h, lanes, :] = ks.T.astype(BF16)
            vn[h, lanes, :] = vs.T.astype(BF16)

        dk_s[h] = jnp.zeros((BAND, seq), F32)
        dv_s[h] = jnp.zeros((BAND, seq), F32)

        @pl.loop(0, line)
        def _(b):
            lanes = pl.ds(pl.multiple_of(b * pair, pair), pair)
            scores = dot(kn[h], xq[h, :, lanes])
            top = jnp.max(scores, axis=0, keepdims=True)
            grown = jnp.exp2((scores - top) * turn)
            inverse = 1.0 / jnp.sum(grown, axis=0, keepdims=True)
            probs = grown * inverse
            probs_all[h, :, lanes] = probs
            attended = dot(xv[h], probs.astype(BF16)).astype(BF16).astype(F32)
            if h == 0:
                att_t[0:BAND, lanes] = attended
            else:
                att_t[72:80, lanes] = attended[8:16]
                att_t[80:144, lanes] = attended[16:80]

    def backward(chip):
        lanes = pl.ds(pl.multiple_of(chip * pair, pair), pair)
        held = og_all[pl.ds(2 * chip, 2)].reshape(pair, width)
        backs = dot(w_mine[...], held, NT)
        if not two:
            backs = jnp.concatenate([backs, jnp.zeros((BAND - span, pair), F32)], axis=0)
        parts = []
        for h in range(per):
            off = 64 * h
            back = jnp.where(owned(h, pair), backs[off:off + BAND], 0.0).astype(BF16)
            delta = jnp.sum(
                back.astype(F32) * att_t[off:off + BAND, lanes], axis=0, keepdims=True
            )
            probs = probs_all[h, :, lanes]
            dprobs = dot(vn[h], back)
            dscores = (probs * (dprobs - delta)).astype(BF16)
            parts.append(dot(xk[h], dscores) * scale)
            dk_s[h] += dot(xq[h, :, lanes], dscores, NT)
            dv_s[h] += dot(back, probs.astype(BF16), NT)
        done = jnp.concatenate([parts[0][0:72], parts[1][8:80]], axis=0) if two else parts[0]
        for j in range(2):
            peer = 2 * chip + j
            block = done[:, j * rows:(j + 1) * rows].astype(BF16)
            ret_q[pl.ds(peer, 1)] = block[None]

            @pl.when(peer != me)
            def _():
                exchange(*set_q, peer, me).start()

    wait_all(*set_a)
    forward(0)
    if not two:
        relay_step(1)
    if line > 2:
        relay_step(2)
    if two:
        wait_all(*set_b)
        forward(1)
    loads[4].wait()
    near = jnp.minimum(z, line - 1 - z)
    toward = jnp.where(z < line - 1 - z, 1, -1)

    @pl.loop(0, line)
    def _(i):
        @pl.when((i >= 2) & (i + 1 < line))
        def _():
            relay_step(i + 1)

        swing = ((i + 1) // 2) * (1 - 2 * lax.rem(i, 2))
        chip = z + jnp.where(i <= 2 * near, swing, toward * (i - near))
        relay(2 * chip + 1 - core, sem_sib.at[chip], sib).wait_recv()
        backward(chip)

    for ref, into, whole, factor in ((dk_s, ret_k, set_k, scale), (dv_s, ret_v, set_v, None)):
        for s in range(n):
            lanes = slice(s * rows, (s + 1) * rows)
            if two:
                part = jnp.concatenate([ref[0, 0:72, lanes], ref[1, 8:80, lanes]], axis=0)
            else:
                part = ref[0, :, lanes]
            if factor is not None:
                part = part * factor
            into[s] = part.astype(BF16)
        send_all(*whole)
    back_q[pl.ds(me, 1)] = ret_q[pl.ds(me, 1)]
    back_k[pl.ds(me, 1)] = ret_k[pl.ds(me, 1)]
    back_v[pl.ds(me, 1)] = ret_v[pl.ds(me, 1)]

    piece = width // ndp
    term = dot(att_t[0:span, :].astype(BF16), og_all[...].reshape(seq, width))
    for j in range(ndp):
        w_out[j, 0:span, :] = term[:, j * piece:(j + 1) * piece].astype(BF16)

    def reduce_copy(peer, slot):
        return pltpu.make_async_remote_copy(
            src_ref=w_out.at[peer],
            dst_ref=w_in.at[slot],
            send_sem=sem_ws.at[peer],
            recv_sem=sem_wr.at[slot],
            device_id={"dp": peer},
            device_id_type=MESH,
        )

    for p in range(1, ndp):
        reduce_copy(lax.rem(dp + p, ndp), dp).start()
    w_in[pl.ds(dp, 1)] = w_out[pl.ds(dp, 1)]

    def unpack(ref, out):
        for d in range(n):
            flip[0, d * span:(d + 1) * span, :] = ref[d].astype(F32)[0:span]
        for g in range(groups):
            out[:, g * rows:(g + 1) * rows] = flip[0, g * rows:(g + 1) * rows, :].T.astype(BF16)

    wait_all(*set_q)
    unpack(back_q, dq_ref)
    for p in range(1, ndp):
        peer = lax.rem(dp + p, ndp)
        reduce_copy(peer, peer).wait_recv()
    result = w_in[0, 0:span, :].astype(F32)
    for j in range(1, ndp):
        result = result + w_in[j, 0:span, :].astype(F32)
    dw_ref[...] = result
    wait_sent(*set_a)
    wait_sent(*set_q)
    if two:
        wait_sent(*set_b)
    for p in range(1, ndp):
        peer = lax.rem(dp + p, ndp)
        reduce_copy(peer, peer).wait_send()
    for part in range(line):
        relay(2 * part + core, sem_sib.at[part], sib).wait_send()

        @pl.when(can_up & (z >= part))
        def _():
            relay(2 * part + core, sem_up.at[part], sib).wait_send()

        @pl.when(can_down & (z <= part))
        def _():
            relay(2 * part + core, sem_down.at[part], sib).wait_send()

    wait_all(*set_k)
    unpack(back_k, dk_ref)
    wait_all(*set_v)
    unpack(back_v, dv_ref)
    wait_sent(*set_k)
    wait_sent(*set_v)


def finish(*refs):
    count = len(refs) // 3
    sources, results, held, sems = refs[:count], refs[count:2 * count], refs[2 * count:-1], refs[-1]
    loads = [pltpu.make_async_copy(sources[i], held[i], sems.at[0, i]) for i in range(count)]
    stores = [pltpu.make_async_copy(held[i], results[i], sems.at[1, i]) for i in range(count)]
    for load in loads:
        load.start()
    for load, store in zip(loads, stores):
        load.wait()
        store.start()
    for store in stores:
        store.wait()


def local(n, ndp, queries, keys, values, out_grad, out_weight, extents):
    rows, width = queries.shape
    per = HEADS // n
    assert per in (1, 2) and rows % 128 == 0
    span = per * HEAD
    padded = -(-span // 16) * 16
    seq = n * rows
    line = n // 2
    images = extents.shape[1]
    if span % 16:
        out_weight = lax.dynamic_slice_in_dim(
            out_weight, lax.axis_index("seq") * span, span, axis=0
        )
    vmem = pl.BlockSpec(memory_space=pltpu.VMEM)
    hbm = pl.BlockSpec(memory_space=pl.ANY)
    grad = jax.ShapeDtypeStruct((rows, width), BF16)
    weight = jax.ShapeDtypeStruct((span, width // ndp), F32)
    dma = pltpu.SemaphoreType.DMA
    buf = pltpu.VMEM
    parts = pl.pallas_call(
        functools.partial(kernel, n, ndp, images),
        out_shape=(grad, grad, grad, weight),
        in_specs=[pl.BlockSpec(memory_space=pltpu.SMEM), hbm, hbm, hbm, hbm, hbm],
        out_specs=(vmem, vmem, vmem, vmem),
        scratch_shapes=[
            buf((rows, width), BF16),
            buf((rows, width), BF16),
            buf((rows, width), BF16),
            buf((n, rows, width), BF16),
            buf((span, width), BF16),
            buf((3, width, rows), F32),
            buf((n, 3 * BAND, rows), BF16),
            buf((n, 3 * 64, rows), BF16),
            buf((n, 3 * BAND, rows), BF16),
            buf((n, 3 * 64, rows), BF16),
            buf((n, padded, rows), BF16),
            buf((n, padded, rows), BF16),
            buf((n, padded, rows), BF16),
            buf((n, padded, rows), BF16),
            buf((n, padded, rows), BF16),
            buf((n, padded, rows), BF16),
            buf((per, BAND, seq), BF16),
            buf((per, BAND, seq), BF16),
            buf((per, BAND, seq), BF16),
            buf((per, seq, BAND), BF16),
            buf((per, seq, BAND), BF16),
            buf((per, seq, seq), F32),
            buf((padded, seq), F32),
            buf((per, BAND, seq), F32),
            buf((per, BAND, seq), F32),
            buf((ndp, padded, width // ndp), BF16),
            buf((ndp, padded, width // ndp), BF16),
        ]
        + [dma((n,))] * 10
        + [dma((n,)), dma((line,)), dma((line,)), dma((line,)), dma((ndp,)), dma((ndp,)), dma((5,))],
        compiler_params=pltpu.CompilerParams(
            collective_id=0, has_side_effects=True, vmem_limit_bytes=56 * 2**20
        ),
        cost_estimate=pl.CostEstimate(
            flops=10 * per * seq * seq * HEAD, bytes_accessed=10 * rows * width * 2,
            transcendentals=per * seq * seq,
        ),
    )(extents, queries, keys, values, out_grad, out_weight)
    return pl.pallas_call(
        finish,
        out_shape=(grad, grad, grad, weight),
        in_specs=[hbm] * 4,
        out_specs=(hbm, hbm, hbm, hbm),
        scratch_shapes=[buf(part.shape, part.dtype) for part in parts] + [dma((2, 4))],
        compiler_params=pltpu.CompilerParams(vmem_limit_bytes=56 * 2**20),
    )(*parts)


def solution(mesh):
    n, ndp = mesh.shape["seq"], mesh.shape["dp"]
    return jax.shard_map(
        functools.partial(local, n, ndp),
        mesh=mesh,
        in_specs=(
            P(("dp", "seq"), None),
            P(("dp", "seq"), None),
            P(("dp", "seq"), None),
            P(("dp", "seq"), None),
            P(),
            P("dp", None),
        ),
        out_specs=(
            P(("dp", "seq"), None),
            P(("dp", "seq"), None),
            P(("dp", "seq"), None),
            P("seq", "dp"),
        ),
        check_vma=False,
    )
```

```python
import functools
import math

import jax
import jax.numpy as jnp
from jax import lax
from jax.experimental import pallas as pl
from jax.experimental.pallas import tpu as pltpu
from jax.sharding import PartitionSpec as P

HEADS = 16
HEAD = 72
UNIT = 64
BAND = 80
FAR = -float(2.0**60)
F32 = jnp.float32
BF16 = jnp.bfloat16
MESH = pl.DeviceIdType.MESH
NT = (((1,), (1,)), ((), ()))
NN = (((1,), (0,)), ((), ()))


def dot(a, b, dims=NN):
    return lax.dot_general(a, b, dims, preferred_element_type=F32)


def kernel(
    n, ndp, images, ext_ref, q_hbm, k_hbm, v_hbm, og_hbm, w_ref,
    dq_ref, dk_ref, dv_ref, dw_ref,
    q_ref, k_ref, v_ref, og_all, w_mine, flip, send_a, send_b, recv_a, recv_b,
    ret_q, ret_k, ret_v, back_q, back_k, back_v,
    xq, xk, xv, kn, vn, grown_all, inverse_all, att_t, dk_s, dv_s, w_out, w_in,
    sem_sa, sem_ra, sem_sb, sem_rb, sem_tq, sem_kq, sem_tk, sem_kk, sem_tv, sem_kv,
    sem_og, sem_up, sem_down, sem_sib, sem_ws, sem_wr, sem_in,
):
    rows, width = q_ref.shape
    per = HEADS // n
    span = per * HEAD
    seq = n * rows
    two = per == 2
    line = n // 2
    pair = 2 * rows
    me = lax.axis_index("seq")
    dp = lax.axis_index("dp")
    z = me // 2
    core = lax.rem(me, 2)
    sib = me + 1 - 2 * core
    groups = width // rows

    if w_ref.shape[0] == span:
        w_from = w_ref
    else:
        w_from = w_ref.at[pl.ds(pl.multiple_of(me * span, span), span), :]
    loads = [
        pltpu.make_async_copy(src, dst, sem_in.at[i])
        for i, (src, dst) in enumerate(
            [(og_hbm, og_all.at[me]), (q_hbm, q_ref), (k_hbm, k_ref), (v_hbm, v_ref), (w_from, w_mine)]
        )
    ]
    for load in loads:
        load.start()

    barrier = pltpu.get_barrier_semaphore()
    for p in range(1, n):
        pl.semaphore_signal(
            barrier, inc=1, device_id={"seq": lax.rem(me + p, n)}, device_id_type=MESH
        )
    for p in range(1, ndp):
        pl.semaphore_signal(
            barrier, inc=1, device_id={"dp": lax.rem(dp + p, ndp)}, device_id_type=MESH
        )

    def relay(src, send_sem, target):
        return pltpu.make_async_remote_copy(
            src_ref=og_all.at[src],
            dst_ref=og_all.at[src],
            send_sem=send_sem,
            recv_sem=sem_og.at[src],
            device_id={"seq": target},
            device_id_type=MESH,
        )

    def exchange(out, into, send_sem, recv_sem, peer, slot):
        return pltpu.make_async_remote_copy(
            src_ref=out.at[peer],
            dst_ref=into.at[slot],
            send_sem=send_sem.at[peer],
            recv_sem=recv_sem.at[slot],
            device_id={"seq": peer},
            device_id_type=MESH,
        )

    def send_all(out, into, send_sem, recv_sem):
        @pl.loop(1, n)
        def _(p):
            exchange(out, into, send_sem, recv_sem, lax.rem(me + p, n), me).start()

    def wait_all(out, into, send_sem, recv_sem):
        @pl.loop(1, n)
        def _(p):
            peer = lax.rem(me + p, n)
            exchange(out, into, send_sem, recv_sem, peer, peer).wait_recv()

    def wait_sent(out, into, send_sem, recv_sem):
        @pl.loop(1, n)
        def _(p):
            peer = lax.rem(me + p, n)
            exchange(out, into, send_sem, recv_sem, peer, peer).wait_send()

    set_a = (send_a, recv_a, sem_sa, sem_ra)
    set_b = (send_b, recv_b, sem_sb, sem_rb)
    set_q = (ret_q, back_q, sem_tq, sem_kq)
    set_k = (ret_k, back_k, sem_tk, sem_kk)
    set_v = (ret_v, back_v, sem_tv, sem_kv)
    can_up = z < line - 1
    can_down = z > 0

    loads[1].wait()
    loads[2].wait()
    loads[3].wait()
    for which, ref in enumerate((q_ref, k_ref, v_ref)):
        for g in range(groups):
            part = ref[:, g * rows:(g + 1) * rows].astype(F32)
            flip[which, g * rows:(g + 1) * rows, :] = part.T
        for d in range(n):
            base = d * span
            if two:
                part = flip[which, base:base + BAND, :]
            else:
                part = jnp.concatenate(
                    [flip[which, base:base + span, :], jnp.zeros((BAND - span, rows), F32)], axis=0
                )
            send_a[d, which * BAND:(which + 1) * BAND, :] = part.astype(BF16)
    loads[0].wait()
    pl.semaphore_wait(barrier, n - 1 + ndp - 1)
    send_all(*set_a)

    @pl.when(can_up)
    def _():
        relay(me, sem_up.at[z], me + 2).start()

    @pl.when(can_down)
    def _():
        relay(me, sem_down.at[z], me - 2).start()

    relay(me, sem_sib.at[z], sib).start()
    recv_a[pl.ds(me, 1)] = send_a[pl.ds(me, 1)]
    def relay_step(step):
        @pl.when(z >= step)
        def _():
            src = me - 2 * step
            relay(src, sem_up.at[z - step], sib).wait_recv()

            @pl.when(can_up)
            def _():
                relay(src, sem_up.at[z - step], me + 2).start()

            relay(src, sem_sib.at[z - step], sib).start()

        @pl.when(z + step < line)
        def _():
            src = me + 2 * step
            relay(src, sem_down.at[z + step], sib).wait_recv()

            @pl.when(can_down)
            def _():
                relay(src, sem_down.at[z + step], me - 2).start()

            relay(src, sem_sib.at[z + step], sib).start()

    if two:
        for which in range(3):
            for d in range(n):
                base = d * span
                send_b[d, which * 64:(which + 1) * 64, :] = flip[
                    which, base + BAND:base + span, :
                ].astype(BF16)
        send_all(*set_b)
        recv_b[pl.ds(me, 1)] = send_b[pl.ds(me, 1)]

    ends = []
    total = jnp.int32(0)
    for i in range(images):
        total = total + ext_ref[0, i] * UNIT
        ends.append(total)

    scale = HEAD ** (-0.5)
    turn = scale * math.log2(math.e)

    def owned(h, lanes):
        row = lax.broadcasted_iota(jnp.int32, (BAND, lanes), 0)
        first = 0 if h == 0 else 8
        return (row >= first) & (row < first + HEAD)

    def forward(h):
        feature = HEAD if h == 0 else 0
        row = lax.broadcasted_iota(jnp.int32, (BAND, rows), 0)
        own = owned(h, rows)
        for s in range(n):
            spot = lax.broadcasted_iota(jnp.int32, (1, rows), 1) + s * rows
            segment = jnp.zeros((1, rows), jnp.int32)
            for end in ends:
                segment = segment + (spot >= end).astype(jnp.int32)
            hit = (row - feature) == segment
            lanes = slice(s * rows, (s + 1) * rows)

            def take(which):
                if h == 0:
                    return recv_a[s, which * BAND:(which + 1) * BAND, :].astype(F32)
                return jnp.concatenate(
                    [
                        recv_a[s, which * BAND + 64:(which + 1) * BAND, :].astype(F32),
                        recv_b[s, which * 64:(which + 1) * 64, :].astype(F32),
                    ],
                    axis=0,
                )

            qs = jnp.where(own, take(0), jnp.where(hit, 1.0, 0.0))
            ks = jnp.where(own, take(1), jnp.where(hit, 0.0, FAR))
            vs = jnp.where(own, take(2), 0.0)
            xq[h, :, lanes] = qs.astype(BF16)
            xk[h, :, lanes] = ks.astype(BF16)
            xv[h, :, lanes] = vs.astype(BF16)
            kn[h, lanes, :] = ks.T.astype(BF16)
            vn[h, lanes, :] = jnp.where(own, take(2), 1.0).T.astype(BF16)

        dk_s[h] = jnp.zeros((BAND, seq), F32)
        dv_s[h] = jnp.zeros((BAND, seq), F32)

        @pl.loop(0, line)
        def _(b):
            lanes = pl.ds(pl.multiple_of(b * pair, pair), pair)
            scores = dot(kn[h], xq[h, :, lanes])
            top = jnp.max(scores, axis=0, keepdims=True)
            grown = jnp.exp2((scores - top) * turn)
            inverse = 1.0 / jnp.sum(grown, axis=0, keepdims=True)
            inverse_all[h, :, lanes] = inverse
            low = grown.astype(BF16)
            grown_all[h, :, lanes] = low
            attended = (dot(xv[h], low) * inverse).astype(BF16).astype(F32)
            if h == 0:
                att_t[0:BAND, lanes] = attended
            else:
                att_t[72:80, lanes] = attended[8:16]
                att_t[80:144, lanes] = attended[16:80]

    def backward(chip):
        lanes = pl.ds(pl.multiple_of(chip * pair, pair), pair)
        held = og_all[pl.ds(2 * chip, 2)].reshape(pair, width)
        backs = dot(w_mine[...], held, NT)
        if not two:
            backs = jnp.concatenate([backs, jnp.zeros((BAND - span, pair), F32)], axis=0)
        parts = []
        for h in range(per):
            off = 64 * h
            extra = HEAD if h == 0 else 0
            back = jnp.where(owned(h, pair), backs[off:off + BAND], 0.0).astype(BF16).astype(F32)
            delta = jnp.sum(back * att_t[off:off + BAND, lanes], axis=0, keepdims=True)
            high = delta.astype(BF16).astype(F32)
            middle = (delta - high).astype(BF16).astype(F32)
            row = lax.broadcasted_iota(jnp.int32, (BAND, pair), 0) - extra
            full = jnp.where(
                row == 0, -high,
                jnp.where(row == 1, -middle, jnp.where(row == 2, high + middle - delta, back)),
            ).astype(BF16)
            inverse = inverse_all[h, :, lanes]
            grown = grown_all[h, :, lanes]
            dscores = (grown.astype(F32) * dot(vn[h], full)).astype(BF16)
            parts.append(dot(xk[h], dscores) * (inverse * scale))
            queries = (xq[h, :, lanes].astype(F32) * inverse).astype(BF16)
            dk_s[h] += dot(queries, dscores, NT)
            dv_s[h] += dot((back * inverse).astype(BF16), grown, NT)
        done = jnp.concatenate([parts[0][0:72], parts[1][8:80]], axis=0) if two else parts[0]
        for j in range(2):
            peer = 2 * chip + j
            block = done[:, j * rows:(j + 1) * rows].astype(BF16)
            ret_q[pl.ds(peer, 1)] = block[None]

            @pl.when(peer != me)
            def _():
                exchange(*set_q, peer, me).start()

    wait_all(*set_a)
    forward(0)
    relay_step(1)
    if two:
        wait_all(*set_b)
        forward(1)
    if line > 2:
        relay_step(2)
    loads[4].wait()
    near = jnp.minimum(z, line - 1 - z)
    toward = jnp.where(z < line - 1 - z, 1, -1)

    @pl.loop(0, line)
    def _(i):
        @pl.when((i >= 2) & (i + 1 < line))
        def _():
            relay_step(i + 1)

        swing = ((i + 1) // 2) * (1 - 2 * lax.rem(i, 2))
        chip = z + jnp.where(i <= 2 * near, swing, toward * (i - near))
        relay(2 * chip + 1 - core, sem_sib.at[chip], sib).wait_recv()
        backward(chip)

    for ref, into, whole, factor in ((dk_s, ret_k, set_k, scale), (dv_s, ret_v, set_v, None)):
        for s in range(n):
            lanes = slice(s * rows, (s + 1) * rows)
            if two:
                part = jnp.concatenate([ref[0, 0:72, lanes], ref[1, 8:80, lanes]], axis=0)
            else:
                part = ref[0, :, lanes]
            if factor is not None:
                part = part * factor
            into[s] = part.astype(BF16)
        send_all(*whole)
    back_q[pl.ds(me, 1)] = ret_q[pl.ds(me, 1)]
    back_k[pl.ds(me, 1)] = ret_k[pl.ds(me, 1)]
    back_v[pl.ds(me, 1)] = ret_v[pl.ds(me, 1)]

    piece = width // ndp
    term = dot(att_t[0:span, :].astype(BF16), og_all[...].reshape(seq, width))
    for j in range(ndp):
        w_out[j, 0:span, :] = term[:, j * piece:(j + 1) * piece].astype(BF16)

    def reduce_copy(peer, slot):
        return pltpu.make_async_remote_copy(
            src_ref=w_out.at[peer],
            dst_ref=w_in.at[slot],
            send_sem=sem_ws.at[peer],
            recv_sem=sem_wr.at[slot],
            device_id={"dp": peer},
            device_id_type=MESH,
        )

    for p in range(1, ndp):
        reduce_copy(lax.rem(dp + p, ndp), dp).start()
    w_in[pl.ds(dp, 1)] = w_out[pl.ds(dp, 1)]

    def unpack(ref, out):
        for d in range(n):
            flip[0, d * span:(d + 1) * span, :] = ref[d].astype(F32)[0:span]
        for g in range(groups):
            out[:, g * rows:(g + 1) * rows] = flip[0, g * rows:(g + 1) * rows, :].T.astype(BF16)

    wait_all(*set_q)
    unpack(back_q, dq_ref)
    for p in range(1, ndp):
        peer = lax.rem(dp + p, ndp)
        reduce_copy(peer, peer).wait_recv()
    result = w_in[0, 0:span, :].astype(F32)
    for j in range(1, ndp):
        result = result + w_in[j, 0:span, :].astype(F32)
    dw_ref[...] = result
    wait_sent(*set_a)
    wait_sent(*set_q)
    if two:
        wait_sent(*set_b)
    for p in range(1, ndp):
        peer = lax.rem(dp + p, ndp)
        reduce_copy(peer, peer).wait_send()
    for part in range(line):
        relay(2 * part + core, sem_sib.at[part], sib).wait_send()

        @pl.when(can_up & (z >= part))
        def _():
            relay(2 * part + core, sem_up.at[part], sib).wait_send()

        @pl.when(can_down & (z <= part))
        def _():
            relay(2 * part + core, sem_down.at[part], sib).wait_send()

    wait_all(*set_k)
    unpack(back_k, dk_ref)
    wait_all(*set_v)
    unpack(back_v, dv_ref)
    wait_sent(*set_k)
    wait_sent(*set_v)


def finish(*refs):
    count = len(refs) // 3
    sources, results, held, sems = refs[:count], refs[count:2 * count], refs[2 * count:-1], refs[-1]
    loads = [pltpu.make_async_copy(sources[i], held[i], sems.at[0, i]) for i in range(count)]
    stores = [pltpu.make_async_copy(held[i], results[i], sems.at[1, i]) for i in range(count)]
    for load in loads:
        load.start()
    for load, store in zip(loads, stores):
        load.wait()
        store.start()
    for store in stores:
        store.wait()


def local(n, ndp, queries, keys, values, out_grad, out_weight, extents):
    rows, width = queries.shape
    per = HEADS // n
    assert per in (1, 2) and rows % 128 == 0
    span = per * HEAD
    padded = -(-span // 16) * 16
    seq = n * rows
    line = n // 2
    images = extents.shape[1]
    if span % 16:
        out_weight = lax.dynamic_slice_in_dim(
            out_weight, lax.axis_index("seq") * span, span, axis=0
        )
    vmem = pl.BlockSpec(memory_space=pltpu.VMEM)
    hbm = pl.BlockSpec(memory_space=pl.ANY)
    grad = jax.ShapeDtypeStruct((rows, width), BF16)
    weight = jax.ShapeDtypeStruct((span, width // ndp), F32)
    dma = pltpu.SemaphoreType.DMA
    buf = pltpu.VMEM
    parts = pl.pallas_call(
        functools.partial(kernel, n, ndp, images),
        out_shape=(grad, grad, grad, weight),
        in_specs=[pl.BlockSpec(memory_space=pltpu.SMEM), hbm, hbm, hbm, hbm, hbm],
        out_specs=(vmem, vmem, vmem, vmem),
        scratch_shapes=[
            buf((rows, width), BF16),
            buf((rows, width), BF16),
            buf((rows, width), BF16),
            buf((n, rows, width), BF16),
            buf((span, width), BF16),
            buf((3, width, rows), F32),
            buf((n, 3 * BAND, rows), BF16),
            buf((n, 3 * 64, rows), BF16),
            buf((n, 3 * BAND, rows), BF16),
            buf((n, 3 * 64, rows), BF16),
            buf((n, padded, rows), BF16),
            buf((n, padded, rows), BF16),
            buf((n, padded, rows), BF16),
            buf((n, padded, rows), BF16),
            buf((n, padded, rows), BF16),
            buf((n, padded, rows), BF16),
            buf((per, BAND, seq), BF16),
            buf((per, BAND, seq), BF16),
            buf((per, BAND, seq), BF16),
            buf((per, seq, BAND), BF16),
            buf((per, seq, BAND), BF16),
            buf((per, seq, seq), BF16),
            buf((per, 1, seq), F32),
            buf((padded, seq), F32),
            buf((per, BAND, seq), F32),
            buf((per, BAND, seq), F32),
            buf((ndp, padded, width // ndp), BF16),
            buf((ndp, padded, width // ndp), BF16),
        ]
        + [dma((n,))] * 10
        + [dma((n,)), dma((line,)), dma((line,)), dma((line,)), dma((ndp,)), dma((ndp,)), dma((5,))],
        compiler_params=pltpu.CompilerParams(
            collective_id=0, has_side_effects=True, vmem_limit_bytes=56 * 2**20
        ),
        cost_estimate=pl.CostEstimate(
            flops=10 * per * seq * seq * HEAD, bytes_accessed=10 * rows * width * 2,
            transcendentals=per * seq * seq,
        ),
    )(extents, queries, keys, values, out_grad, out_weight)
    return pl.pallas_call(
        finish,
        out_shape=(grad, grad, grad, weight),
        in_specs=[hbm] * 4,
        out_specs=(hbm, hbm, hbm, hbm),
        scratch_shapes=[buf(part.shape, part.dtype) for part in parts] + [dma((2, 4))],
        compiler_params=pltpu.CompilerParams(vmem_limit_bytes=56 * 2**20),
    )(*parts)


def solution(mesh):
    n, ndp = mesh.shape["seq"], mesh.shape["dp"]
    return jax.shard_map(
        functools.partial(local, n, ndp),
        mesh=mesh,
        in_specs=(
            P(("dp", "seq"), None),
            P(("dp", "seq"), None),
            P(("dp", "seq"), None),
            P(("dp", "seq"), None),
            P(),
            P("dp", None),
        ),
        out_specs=(
            P(("dp", "seq"), None),
            P(("dp", "seq"), None),
            P(("dp", "seq"), None),
            P("seq", "dp"),
        ),
        check_vma=False,
    )
```

```python
import functools
import math

import jax
import jax.numpy as jnp
from jax import lax
from jax.experimental import pallas as pl
from jax.experimental.pallas import tpu as pltpu
from jax.sharding import PartitionSpec as P

HEADS = 16
HEAD = 72
UNIT = 64
BAND = 80
FAR = -float(2.0**60)
F32 = jnp.float32
BF16 = jnp.bfloat16
MESH = pl.DeviceIdType.MESH
NT = (((1,), (1,)), ((), ()))
NN = (((1,), (0,)), ((), ()))


def dot(a, b, dims=NN):
    return lax.dot_general(a, b, dims, preferred_element_type=F32)


def kernel(
    n, ndp, images, ext_ref, q_hbm, k_hbm, v_hbm, og_hbm, w_ref,
    dq_ref, dk_ref, dv_ref, dw_ref,
    q_ref, k_ref, v_ref, og_all, w_mine, flip, send_a, send_b, recv_a, recv_b,
    ret_q, ret_k, ret_v, back_q, back_k, back_v,
    xq, xk, xv, kn, vn, grown_all, inverse_all, att_t, dk_s, dv_s, w_out, w_in,
    sem_sa, sem_ra, sem_sb, sem_rb, sem_tq, sem_kq, sem_tk, sem_kk, sem_tv, sem_kv,
    sem_og, sem_up, sem_down, sem_sib, sem_ws, sem_wr, sem_in,
):
    rows, width = q_ref.shape
    per = HEADS // n
    span = per * HEAD
    seq = n * rows
    two = per == 2
    line = n // 2
    pair = 2 * rows
    me = lax.axis_index("seq")
    dp = lax.axis_index("dp")
    z = me // 2
    core = lax.rem(me, 2)
    sib = me + 1 - 2 * core
    groups = width // rows

    if w_ref.shape[0] == span:
        w_from = w_ref
    else:
        w_from = w_ref.at[pl.ds(pl.multiple_of(me * span, span), span), :]
    loads = [
        pltpu.make_async_copy(src, dst, sem_in.at[i])
        for i, (src, dst) in enumerate(
            [(og_hbm, og_all.at[me]), (q_hbm, q_ref), (k_hbm, k_ref), (v_hbm, v_ref), (w_from, w_mine)]
        )
    ]
    for load in loads:
        load.start()

    barrier = pltpu.get_barrier_semaphore()
    for p in range(1, n):
        pl.semaphore_signal(
            barrier, inc=1, device_id={"seq": lax.rem(me + p, n)}, device_id_type=MESH
        )
    for p in range(1, ndp):
        pl.semaphore_signal(
            barrier, inc=1, device_id={"dp": lax.rem(dp + p, ndp)}, device_id_type=MESH
        )

    def relay(src, send_sem, target):
        return pltpu.make_async_remote_copy(
            src_ref=og_all.at[src],
            dst_ref=og_all.at[src],
            send_sem=send_sem,
            recv_sem=sem_og.at[src],
            device_id={"seq": target},
            device_id_type=MESH,
        )

    def exchange(out, into, send_sem, recv_sem, peer, slot):
        return pltpu.make_async_remote_copy(
            src_ref=out.at[peer],
            dst_ref=into.at[slot],
            send_sem=send_sem.at[peer],
            recv_sem=recv_sem.at[slot],
            device_id={"seq": peer},
            device_id_type=MESH,
        )

    def send_all(out, into, send_sem, recv_sem):
        @pl.loop(1, n)
        def _(p):
            step = jnp.where(p <= n // 2, n // 2 + p - 1, p - n // 2)
            exchange(out, into, send_sem, recv_sem, lax.rem(me + step, n), me).start()

    def wait_all(out, into, send_sem, recv_sem):
        @pl.loop(1, n)
        def _(p):
            peer = lax.rem(me + p, n)
            exchange(out, into, send_sem, recv_sem, peer, peer).wait_recv()

    def wait_sent(out, into, send_sem, recv_sem):
        @pl.loop(1, n)
        def _(p):
            peer = lax.rem(me + p, n)
            exchange(out, into, send_sem, recv_sem, peer, peer).wait_send()

    set_a = (send_a, recv_a, sem_sa, sem_ra)
    set_b = (send_b, recv_b, sem_sb, sem_rb)
    set_q = (ret_q, back_q, sem_tq, sem_kq)
    set_k = (ret_k, back_k, sem_tk, sem_kk)
    set_v = (ret_v, back_v, sem_tv, sem_kv)
    can_up = z < line - 1
    can_down = z > 0

    loads[1].wait()
    loads[2].wait()
    loads[3].wait()
    for which, ref in enumerate((q_ref, k_ref, v_ref)):
        for g in range(groups):
            part = ref[:, g * rows:(g + 1) * rows].astype(F32)
            flip[which, g * rows:(g + 1) * rows, :] = part.T
        for d in range(n):
            base = d * span
            if two:
                part = flip[which, base:base + BAND, :]
            else:
                part = jnp.concatenate(
                    [flip[which, base:base + span, :], jnp.zeros((BAND - span, rows), F32)], axis=0
                )
            send_a[d, which * BAND:(which + 1) * BAND, :] = part.astype(BF16)
    loads[0].wait()
    pl.semaphore_wait(barrier, n - 1 + ndp - 1)
    send_all(*set_a)

    @pl.when(can_up)
    def _():
        relay(me, sem_up.at[z], me + 2).start()

    @pl.when(can_down)
    def _():
        relay(me, sem_down.at[z], me - 2).start()

    relay(me, sem_sib.at[z], sib).start()
    recv_a[pl.ds(me, 1)] = send_a[pl.ds(me, 1)]
    def relay_step(step):
        @pl.when(z >= step)
        def _():
            src = me - 2 * step
            relay(src, sem_up.at[z - step], sib).wait_recv()

            @pl.when(can_up)
            def _():
                relay(src, sem_up.at[z - step], me + 2).start()

            relay(src, sem_sib.at[z - step], sib).start()

        @pl.when(z + step < line)
        def _():
            src = me + 2 * step
            relay(src, sem_down.at[z + step], sib).wait_recv()

            @pl.when(can_down)
            def _():
                relay(src, sem_down.at[z + step], me - 2).start()

            relay(src, sem_sib.at[z + step], sib).start()

    if two:
        for which in range(3):
            for d in range(n):
                base = d * span
                send_b[d, which * 64:(which + 1) * 64, :] = flip[
                    which, base + BAND:base + span, :
                ].astype(BF16)
        send_all(*set_b)
        recv_b[pl.ds(me, 1)] = send_b[pl.ds(me, 1)]

    ends = []
    total = jnp.int32(0)
    for i in range(images):
        total = total + ext_ref[0, i] * UNIT
        ends.append(total)

    scale = HEAD ** (-0.5)
    turn = scale * math.log2(math.e)

    def owned(h, lanes):
        row = lax.broadcasted_iota(jnp.int32, (BAND, lanes), 0)
        first = 0 if h == 0 else 8
        return (row >= first) & (row < first + HEAD)

    def forward(h):
        feature = HEAD if h == 0 else 0
        row = lax.broadcasted_iota(jnp.int32, (BAND, rows), 0)
        own = owned(h, rows)
        for s in range(n):
            spot = lax.broadcasted_iota(jnp.int32, (1, rows), 1) + s * rows
            segment = jnp.zeros((1, rows), jnp.int32)
            for end in ends:
                segment = segment + (spot >= end).astype(jnp.int32)
            hit = (row - feature) == segment
            lanes = slice(s * rows, (s + 1) * rows)

            def take(which):
                if h == 0:
                    return recv_a[s, which * BAND:(which + 1) * BAND, :].astype(F32)
                return jnp.concatenate(
                    [
                        recv_a[s, which * BAND + 64:(which + 1) * BAND, :].astype(F32),
                        recv_b[s, which * 64:(which + 1) * 64, :].astype(F32),
                    ],
                    axis=0,
                )

            qs = jnp.where(own, take(0), jnp.where(hit, 1.0, 0.0))
            ks = jnp.where(own, take(1), jnp.where(hit, 0.0, FAR))
            vs = jnp.where(own, take(2), 0.0)
            xq[h, :, lanes] = qs.astype(BF16)
            xk[h, :, lanes] = ks.astype(BF16)
            xv[h, :, lanes] = vs.astype(BF16)
            kn[h, lanes, :] = ks.T.astype(BF16)
            vn[h, lanes, :] = jnp.where(own, take(2), 1.0).T.astype(BF16)

        dk_s[h] = jnp.zeros((BAND, seq), F32)
        dv_s[h] = jnp.zeros((BAND, seq), F32)

        @pl.loop(0, line)
        def _(b):
            lanes = pl.ds(pl.multiple_of(b * pair, pair), pair)
            scores = dot(kn[h], xq[h, :, lanes])
            top = jnp.max(scores, axis=0, keepdims=True)
            grown = jnp.exp2((scores - top) * turn)
            inverse = 1.0 / jnp.sum(grown, axis=0, keepdims=True)
            inverse_all[h, :, lanes] = inverse
            low = grown.astype(BF16)
            grown_all[h, :, lanes] = low
            attended = (dot(xv[h], low) * inverse).astype(BF16).astype(F32)
            if h == 0:
                att_t[0:BAND, lanes] = attended
            else:
                att_t[72:80, lanes] = attended[8:16]
                att_t[80:144, lanes] = attended[16:80]

    def backward(chip):
        lanes = pl.ds(pl.multiple_of(chip * pair, pair), pair)
        held = og_all[pl.ds(2 * chip, 2)].reshape(pair, width)
        backs = dot(w_mine[...], held, NT)
        if not two:
            backs = jnp.concatenate([backs, jnp.zeros((BAND - span, pair), F32)], axis=0)
        parts = []
        for h in range(per):
            off = 64 * h
            extra = HEAD if h == 0 else 0
            back = jnp.where(owned(h, pair), backs[off:off + BAND], 0.0).astype(BF16).astype(F32)
            delta = jnp.sum(back * att_t[off:off + BAND, lanes], axis=0, keepdims=True)
            high = delta.astype(BF16).astype(F32)
            middle = (delta - high).astype(BF16).astype(F32)
            row = lax.broadcasted_iota(jnp.int32, (BAND, pair), 0) - extra
            full = jnp.where(
                row == 0, -high,
                jnp.where(row == 1, -middle, jnp.where(row == 2, high + middle - delta, back)),
            ).astype(BF16)
            inverse = inverse_all[h, :, lanes]
            grown = grown_all[h, :, lanes]
            dscores = (grown.astype(F32) * dot(vn[h], full)).astype(BF16)
            parts.append(dot(xk[h], dscores) * (inverse * scale))
            queries = (xq[h, :, lanes].astype(F32) * inverse).astype(BF16)
            dk_s[h] += dot(queries, dscores, NT)
            dv_s[h] += dot((back * inverse).astype(BF16), grown, NT)
        done = jnp.concatenate([parts[0][0:72], parts[1][8:80]], axis=0) if two else parts[0]
        for j in range(2):
            peer = 2 * chip + j
            block = done[:, j * rows:(j + 1) * rows].astype(BF16)
            ret_q[pl.ds(peer, 1)] = block[None]

            @pl.when(peer != me)
            def _():
                exchange(*set_q, peer, me).start()

    wait_all(*set_a)
    forward(0)
    relay_step(1)
    if line > 2:
        relay_step(2)
    if two:
        wait_all(*set_b)
        forward(1)
    loads[4].wait()
    near = jnp.minimum(z, line - 1 - z)
    toward = jnp.where(z < line - 1 - z, 1, -1)

    @pl.loop(0, line)
    def _(i):
        @pl.when((i >= 2) & (i + 1 < line))
        def _():
            relay_step(i + 1)

        swing = ((i + 1) // 2) * (1 - 2 * lax.rem(i, 2))
        chip = z + jnp.where(i <= 2 * near, swing, toward * (i - near))
        relay(2 * chip + 1 - core, sem_sib.at[chip], sib).wait_recv()
        backward(chip)

    for ref, into, whole, factor in ((dk_s, ret_k, set_k, scale), (dv_s, ret_v, set_v, None)):
        for s in range(n):
            lanes = slice(s * rows, (s + 1) * rows)
            if two:
                part = jnp.concatenate([ref[0, 0:72, lanes], ref[1, 8:80, lanes]], axis=0)
            else:
                part = ref[0, :, lanes]
            if factor is not None:
                part = part * factor
            into[s] = part.astype(BF16)
        send_all(*whole)
    back_q[pl.ds(me, 1)] = ret_q[pl.ds(me, 1)]
    back_k[pl.ds(me, 1)] = ret_k[pl.ds(me, 1)]
    back_v[pl.ds(me, 1)] = ret_v[pl.ds(me, 1)]

    piece = width // ndp
    term = dot(att_t[0:span, :].astype(BF16), og_all[...].reshape(seq, width))
    for j in range(ndp):
        w_out[j, 0:span, :] = term[:, j * piece:(j + 1) * piece].astype(BF16)

    def reduce_copy(peer, slot):
        return pltpu.make_async_remote_copy(
            src_ref=w_out.at[peer],
            dst_ref=w_in.at[slot],
            send_sem=sem_ws.at[peer],
            recv_sem=sem_wr.at[slot],
            device_id={"dp": peer},
            device_id_type=MESH,
        )

    for p in range(1, ndp):
        reduce_copy(lax.rem(dp + p, ndp), dp).start()
    w_in[pl.ds(dp, 1)] = w_out[pl.ds(dp, 1)]

    def unpack(ref, out):
        for d in range(n):
            flip[0, d * span:(d + 1) * span, :] = ref[d].astype(F32)[0:span]
        for g in range(groups):
            out[:, g * rows:(g + 1) * rows] = flip[0, g * rows:(g + 1) * rows, :].T.astype(BF16)

    wait_all(*set_q)
    unpack(back_q, dq_ref)
    for p in range(1, ndp):
        peer = lax.rem(dp + p, ndp)
        reduce_copy(peer, peer).wait_recv()
    result = w_in[0, 0:span, :].astype(F32)
    for j in range(1, ndp):
        result = result + w_in[j, 0:span, :].astype(F32)
    dw_ref[...] = result
    wait_sent(*set_a)
    wait_sent(*set_q)
    if two:
        wait_sent(*set_b)
    for p in range(1, ndp):
        peer = lax.rem(dp + p, ndp)
        reduce_copy(peer, peer).wait_send()
    for part in range(line):
        relay(2 * part + core, sem_sib.at[part], sib).wait_send()

        @pl.when(can_up & (z >= part))
        def _():
            relay(2 * part + core, sem_up.at[part], sib).wait_send()

        @pl.when(can_down & (z <= part))
        def _():
            relay(2 * part + core, sem_down.at[part], sib).wait_send()

    wait_all(*set_k)
    unpack(back_k, dk_ref)
    wait_all(*set_v)
    unpack(back_v, dv_ref)
    wait_sent(*set_k)
    wait_sent(*set_v)


def finish(*refs):
    count = len(refs) // 3
    sources, results, held, sems = refs[:count], refs[count:2 * count], refs[2 * count:-1], refs[-1]
    loads = [pltpu.make_async_copy(sources[i], held[i], sems.at[0, i]) for i in range(count)]
    stores = [pltpu.make_async_copy(held[i], results[i], sems.at[1, i]) for i in range(count)]
    for load in loads:
        load.start()
    for load, store in zip(loads, stores):
        load.wait()
        store.start()
    for store in stores:
        store.wait()


def local(n, ndp, queries, keys, values, out_grad, out_weight, extents):
    rows, width = queries.shape
    per = HEADS // n
    assert per in (1, 2) and rows % 128 == 0
    span = per * HEAD
    padded = -(-span // 16) * 16
    seq = n * rows
    line = n // 2
    images = extents.shape[1]
    if span % 16:
        out_weight = lax.dynamic_slice_in_dim(
            out_weight, lax.axis_index("seq") * span, span, axis=0
        )
    vmem = pl.BlockSpec(memory_space=pltpu.VMEM)
    hbm = pl.BlockSpec(memory_space=pl.ANY)
    grad = jax.ShapeDtypeStruct((rows, width), BF16)
    weight = jax.ShapeDtypeStruct((span, width // ndp), F32)
    dma = pltpu.SemaphoreType.DMA
    buf = pltpu.VMEM
    parts = pl.pallas_call(
        functools.partial(kernel, n, ndp, images),
        out_shape=(grad, grad, grad, weight),
        in_specs=[pl.BlockSpec(memory_space=pltpu.SMEM), hbm, hbm, hbm, hbm, hbm],
        out_specs=(vmem, vmem, vmem, vmem),
        scratch_shapes=[
            buf((rows, width), BF16),
            buf((rows, width), BF16),
            buf((rows, width), BF16),
            buf((n, rows, width), BF16),
            buf((span, width), BF16),
            buf((3, width, rows), F32),
            buf((n, 3 * BAND, rows), BF16),
            buf((n, 3 * 64, rows), BF16),
            buf((n, 3 * BAND, rows), BF16),
            buf((n, 3 * 64, rows), BF16),
            buf((n, padded, rows), BF16),
            buf((n, padded, rows), BF16),
            buf((n, padded, rows), BF16),
            buf((n, padded, rows), BF16),
            buf((n, padded, rows), BF16),
            buf((n, padded, rows), BF16),
            buf((per, BAND, seq), BF16),
            buf((per, BAND, seq), BF16),
            buf((per, BAND, seq), BF16),
            buf((per, seq, BAND), BF16),
            buf((per, seq, BAND), BF16),
            buf((per, seq, seq), BF16),
            buf((per, 1, seq), F32),
            buf((padded, seq), F32),
            buf((per, BAND, seq), F32),
            buf((per, BAND, seq), F32),
            buf((ndp, padded, width // ndp), BF16),
            buf((ndp, padded, width // ndp), BF16),
        ]
        + [dma((n,))] * 10
        + [dma((n,)), dma((line,)), dma((line,)), dma((line,)), dma((ndp,)), dma((ndp,)), dma((5,))],
        compiler_params=pltpu.CompilerParams(
            collective_id=0, has_side_effects=True, vmem_limit_bytes=56 * 2**20
        ),
        cost_estimate=pl.CostEstimate(
            flops=10 * per * seq * seq * HEAD, bytes_accessed=10 * rows * width * 2,
            transcendentals=per * seq * seq,
        ),
    )(extents, queries, keys, values, out_grad, out_weight)
    return pl.pallas_call(
        finish,
        out_shape=(grad, grad, grad, weight),
        in_specs=[hbm] * 4,
        out_specs=(hbm, hbm, hbm, hbm),
        scratch_shapes=[buf(part.shape, part.dtype) for part in parts] + [dma((2, 4))],
        compiler_params=pltpu.CompilerParams(vmem_limit_bytes=56 * 2**20),
    )(*parts)


def solution(mesh):
    n, ndp = mesh.shape["seq"], mesh.shape["dp"]
    return jax.shard_map(
        functools.partial(local, n, ndp),
        mesh=mesh,
        in_specs=(
            P(("dp", "seq"), None),
            P(("dp", "seq"), None),
            P(("dp", "seq"), None),
            P(("dp", "seq"), None),
            P(),
            P("dp", None),
        ),
        out_specs=(
            P(("dp", "seq"), None),
            P(("dp", "seq"), None),
            P(("dp", "seq"), None),
            P("seq", "dp"),
        ),
        check_vma=False,
    )
```

```python
import functools
import math

import jax
import jax.numpy as jnp
from jax import lax
from jax.experimental import pallas as pl
from jax.experimental.pallas import tpu as pltpu
from jax.sharding import PartitionSpec as P

HEADS = 16
HEAD = 72
UNIT = 64
BAND = 80
FAR = -float(2.0**60)
F32 = jnp.float32
BF16 = jnp.bfloat16
MESH = pl.DeviceIdType.MESH
NT = (((1,), (1,)), ((), ()))
NN = (((1,), (0,)), ((), ()))


def dot(a, b, dims=NN):
    return lax.dot_general(a, b, dims, preferred_element_type=F32)


def kernel(
    n, ndp, images, ext_ref, q_hbm, k_hbm, v_hbm, og_hbm, w_ref,
    dq_ref, dk_ref, dv_ref, dw_ref,
    q_ref, k_ref, v_ref, og_all, w_mine, flip, send_a, send_b, recv_a, recv_b,
    ret_q, ret_k, ret_v, back_q, back_k, back_v,
    xq, xk, xv, kn, vn, grown_all, inverse_all, att_t, dk_s, dv_s, w_out, w_in,
    sem_sa, sem_ra, sem_sb, sem_rb, sem_tq, sem_kq, sem_tk, sem_kk, sem_tv, sem_kv,
    sem_og, sem_up, sem_down, sem_sib, sem_ws, sem_wr, sem_in,
):
    rows, width = q_ref.shape
    per = HEADS // n
    span = per * HEAD
    seq = n * rows
    two = per == 2
    line = n // 2
    pair = 2 * rows
    me = lax.axis_index("seq")
    dp = lax.axis_index("dp")
    z = me // 2
    core = lax.rem(me, 2)
    sib = me + 1 - 2 * core
    groups = width // rows

    if w_ref.shape[0] == span:
        w_from = w_ref
    else:
        w_from = w_ref.at[pl.ds(pl.multiple_of(me * span, span), span), :]
    loads = [
        pltpu.make_async_copy(src, dst, sem_in.at[i])
        for i, (src, dst) in enumerate(
            [(og_hbm, og_all.at[me]), (q_hbm, q_ref), (k_hbm, k_ref), (v_hbm, v_ref), (w_from, w_mine)]
        )
    ]
    for load in loads:
        load.start()

    barrier = pltpu.get_barrier_semaphore()
    for p in range(1, n):
        pl.semaphore_signal(
            barrier, inc=1, device_id={"seq": lax.rem(me + p, n)}, device_id_type=MESH
        )
    for p in range(1, ndp):
        pl.semaphore_signal(
            barrier, inc=1, device_id={"dp": lax.rem(dp + p, ndp)}, device_id_type=MESH
        )

    def relay(src, send_sem, target):
        return pltpu.make_async_remote_copy(
            src_ref=og_all.at[src],
            dst_ref=og_all.at[src],
            send_sem=send_sem,
            recv_sem=sem_og.at[src],
            device_id={"seq": target},
            device_id_type=MESH,
        )

    def exchange(out, into, send_sem, recv_sem, peer, slot):
        return pltpu.make_async_remote_copy(
            src_ref=out.at[peer],
            dst_ref=into.at[slot],
            send_sem=send_sem.at[peer],
            recv_sem=recv_sem.at[slot],
            device_id={"seq": peer},
            device_id_type=MESH,
        )

    def send_all(out, into, send_sem, recv_sem):
        @pl.loop(1, n)
        def _(p):
            exchange(out, into, send_sem, recv_sem, lax.rem(me + p, n), me).start()

    def wait_all(out, into, send_sem, recv_sem):
        @pl.loop(1, n)
        def _(p):
            peer = lax.rem(me + p, n)
            exchange(out, into, send_sem, recv_sem, peer, peer).wait_recv()

    def wait_sent(out, into, send_sem, recv_sem):
        @pl.loop(1, n)
        def _(p):
            peer = lax.rem(me + p, n)
            exchange(out, into, send_sem, recv_sem, peer, peer).wait_send()

    set_a = (send_a, recv_a, sem_sa, sem_ra)
    set_b = (send_b, recv_b, sem_sb, sem_rb)
    set_q = (ret_q, back_q, sem_tq, sem_kq)
    set_k = (ret_k, back_k, sem_tk, sem_kk)
    set_v = (ret_v, back_v, sem_tv, sem_kv)
    can_up = z < line - 1
    can_down = z > 0

    loads[1].wait()
    loads[2].wait()
    loads[3].wait()
    for which, ref in enumerate((q_ref, k_ref, v_ref)):
        for g in range(groups):
            part = ref[:, g * rows:(g + 1) * rows].astype(F32)
            flip[which, g * rows:(g + 1) * rows, :] = part.T
        for d in range(n):
            base = d * span
            if two:
                part = flip[which, base:base + BAND, :]
            else:
                part = jnp.concatenate(
                    [flip[which, base:base + span, :], jnp.zeros((BAND - span, rows), F32)], axis=0
                )
            send_a[d, which * BAND:(which + 1) * BAND, :] = part.astype(BF16)
    loads[0].wait()
    pl.semaphore_wait(barrier, n - 1 + ndp - 1)
    send_all(*set_a)

    @pl.when(can_up)
    def _():
        relay(me, sem_up.at[z], me + 2).start()

    @pl.when(can_down)
    def _():
        relay(me, sem_down.at[z], me - 2).start()

    relay(me, sem_sib.at[z], sib).start()
    recv_a[pl.ds(me, 1)] = send_a[pl.ds(me, 1)]
    def relay_step(step):
        @pl.when(z >= step)
        def _():
            src = me - 2 * step
            relay(src, sem_up.at[z - step], sib).wait_recv()

            @pl.when(can_up)
            def _():
                relay(src, sem_up.at[z - step], me + 2).start()

            relay(src, sem_sib.at[z - step], sib).start()

        @pl.when(z + step < line)
        def _():
            src = me + 2 * step
            relay(src, sem_down.at[z + step], sib).wait_recv()

            @pl.when(can_down)
            def _():
                relay(src, sem_down.at[z + step], me - 2).start()

            relay(src, sem_sib.at[z + step], sib).start()

    if two:
        for which in range(3):
            for d in range(n):
                base = d * span
                send_b[d, which * 64:(which + 1) * 64, :] = flip[
                    which, base + BAND:base + span, :
                ].astype(BF16)
        send_all(*set_b)
        recv_b[pl.ds(me, 1)] = send_b[pl.ds(me, 1)]

    ends = []
    total = jnp.int32(0)
    for i in range(images):
        total = total + ext_ref[0, i] * UNIT
        ends.append(total)

    scale = HEAD ** (-0.5)
    turn = scale * math.log2(math.e)

    def owned(h, lanes):
        row = lax.broadcasted_iota(jnp.int32, (BAND, lanes), 0)
        first = 0 if h == 0 else 8
        return (row >= first) & (row < first + HEAD)

    def forward(h):
        feature = HEAD if h == 0 else 0
        row = lax.broadcasted_iota(jnp.int32, (BAND, rows), 0)
        own = owned(h, rows)
        for s in range(n):
            spot = lax.broadcasted_iota(jnp.int32, (1, rows), 1) + s * rows
            segment = jnp.zeros((1, rows), jnp.int32)
            for end in ends:
                segment = segment + (spot >= end).astype(jnp.int32)
            hit = (row - feature) == segment
            lanes = slice(s * rows, (s + 1) * rows)

            def take(which):
                if h == 0:
                    return recv_a[s, which * BAND:(which + 1) * BAND, :].astype(F32)
                return jnp.concatenate(
                    [
                        recv_a[s, which * BAND + 64:(which + 1) * BAND, :].astype(F32),
                        recv_b[s, which * 64:(which + 1) * 64, :].astype(F32),
                    ],
                    axis=0,
                )

            qs = jnp.where(own, take(0), jnp.where(hit, 1.0, 0.0))
            ks = jnp.where(own, take(1), jnp.where(hit, 0.0, FAR))
            vs = jnp.where(own, take(2), 0.0)
            xq[h, :, lanes] = qs.astype(BF16)
            xk[h, :, lanes] = ks.astype(BF16)
            xv[h, :, lanes] = vs.astype(BF16)
            kn[h, lanes, :] = ks.T.astype(BF16)
            vn[h, lanes, :] = jnp.where(own, take(2), 1.0).T.astype(BF16)

        dk_s[h] = jnp.zeros((BAND, seq), F32)
        dv_s[h] = jnp.zeros((BAND, seq), F32)

        @pl.loop(0, line)
        def _(b):
            lanes = pl.ds(pl.multiple_of(b * pair, pair), pair)
            scores = dot(kn[h], xq[h, :, lanes])
            top = jnp.max(scores, axis=0, keepdims=True)
            grown = jnp.exp2((scores - top) * turn)
            inverse = 1.0 / jnp.sum(grown, axis=0, keepdims=True)
            inverse_all[h, :, lanes] = inverse
            low = grown.astype(BF16)
            grown_all[h, :, lanes] = low
            attended = (dot(xv[h], low) * inverse).astype(BF16).astype(F32)
            if h == 0:
                att_t[0:BAND, lanes] = attended
            else:
                att_t[72:80, lanes] = attended[8:16]
                att_t[80:144, lanes] = attended[16:80]

    def backward(chip):
        lanes = pl.ds(pl.multiple_of(chip * pair, pair), pair)
        held = og_all[pl.ds(2 * chip, 2)].reshape(pair, width)
        backs = dot(w_mine[...], held, NT)
        if not two:
            backs = jnp.concatenate([backs, jnp.zeros((BAND - span, pair), F32)], axis=0)
        parts = []
        for h in range(per):
            off = 64 * h
            extra = HEAD if h == 0 else 0
            back = jnp.where(owned(h, pair), backs[off:off + BAND], 0.0).astype(BF16).astype(F32)
            delta = jnp.sum(back * att_t[off:off + BAND, lanes], axis=0, keepdims=True)
            high = delta.astype(BF16).astype(F32)
            middle = (delta - high).astype(BF16).astype(F32)
            row = lax.broadcasted_iota(jnp.int32, (BAND, pair), 0) - extra
            full = jnp.where(
                row == 0, -high,
                jnp.where(row == 1, -middle, jnp.where(row == 2, high + middle - delta, back)),
            ).astype(BF16)
            inverse = inverse_all[h, :, lanes]
            grown = grown_all[h, :, lanes]
            dscores = (grown.astype(F32) * dot(vn[h], full)).astype(BF16)
            parts.append(dot(xk[h], dscores) * (inverse * scale))
            queries = (xq[h, :, lanes].astype(F32) * inverse).astype(BF16)
            dk_s[h] += dot(queries, dscores, NT)
            dv_s[h] += dot((back * inverse).astype(BF16), grown, NT)
        done = jnp.concatenate([parts[0][0:72], parts[1][8:80]], axis=0) if two else parts[0]
        for j in range(2):
            peer = 2 * chip + j
            block = done[:, j * rows:(j + 1) * rows].astype(BF16)
            ret_q[pl.ds(peer, 1)] = block[None]

            @pl.when(peer != me)
            def _():
                exchange(*set_q, peer, me).start()

    wait_all(*set_a)
    forward(0)
    relay_step(1)
    if two:
        wait_all(*set_b)
        forward(1)
    loads[4].wait()
    near = jnp.minimum(z, line - 1 - z)
    toward = jnp.where(z < line - 1 - z, 1, -1)

    @pl.loop(0, line)
    def _(i):
        @pl.when((i >= 1) & (i + 1 < line))
        def _():
            relay_step(i + 1)

        swing = ((i + 1) // 2) * (1 - 2 * lax.rem(i, 2))
        chip = z + jnp.where(i <= 2 * near, swing, toward * (i - near))
        relay(2 * chip + 1 - core, sem_sib.at[chip], sib).wait_recv()
        backward(chip)

    for ref, into, whole, factor in ((dk_s, ret_k, set_k, scale), (dv_s, ret_v, set_v, None)):
        for s in range(n):
            lanes = slice(s * rows, (s + 1) * rows)
            if two:
                part = jnp.concatenate([ref[0, 0:72, lanes], ref[1, 8:80, lanes]], axis=0)
            else:
                part = ref[0, :, lanes]
            if factor is not None:
                part = part * factor
            into[s] = part.astype(BF16)
        send_all(*whole)
    back_q[pl.ds(me, 1)] = ret_q[pl.ds(me, 1)]
    back_k[pl.ds(me, 1)] = ret_k[pl.ds(me, 1)]
    back_v[pl.ds(me, 1)] = ret_v[pl.ds(me, 1)]

    piece = width // ndp
    term = dot(att_t[0:span, :].astype(BF16), og_all[...].reshape(seq, width))
    for j in range(ndp):
        w_out[j, 0:span, :] = term[:, j * piece:(j + 1) * piece].astype(BF16)

    def reduce_copy(peer, slot):
        return pltpu.make_async_remote_copy(
            src_ref=w_out.at[peer],
            dst_ref=w_in.at[slot],
            send_sem=sem_ws.at[peer],
            recv_sem=sem_wr.at[slot],
            device_id={"dp": peer},
            device_id_type=MESH,
        )

    for p in range(1, ndp):
        reduce_copy(lax.rem(dp + p, ndp), dp).start()
    w_in[pl.ds(dp, 1)] = w_out[pl.ds(dp, 1)]

    def unpack(ref, out):
        for d in range(n):
            flip[0, d * span:(d + 1) * span, :] = ref[d].astype(F32)[0:span]
        for g in range(groups):
            out[:, g * rows:(g + 1) * rows] = flip[0, g * rows:(g + 1) * rows, :].T.astype(BF16)

    wait_all(*set_q)
    unpack(back_q, dq_ref)
    for p in range(1, ndp):
        peer = lax.rem(dp + p, ndp)
        reduce_copy(peer, peer).wait_recv()
    result = w_in[0, 0:span, :].astype(F32)
    for j in range(1, ndp):
        result = result + w_in[j, 0:span, :].astype(F32)
    dw_ref[...] = result
    wait_sent(*set_a)
    wait_sent(*set_q)
    if two:
        wait_sent(*set_b)
    for p in range(1, ndp):
        peer = lax.rem(dp + p, ndp)
        reduce_copy(peer, peer).wait_send()
    for part in range(line):
        relay(2 * part + core, sem_sib.at[part], sib).wait_send()

        @pl.when(can_up & (z >= part))
        def _():
            relay(2 * part + core, sem_up.at[part], sib).wait_send()

        @pl.when(can_down & (z <= part))
        def _():
            relay(2 * part + core, sem_down.at[part], sib).wait_send()

    wait_all(*set_k)
    unpack(back_k, dk_ref)
    wait_all(*set_v)
    unpack(back_v, dv_ref)
    wait_sent(*set_k)
    wait_sent(*set_v)


def finish(*refs):
    count = len(refs) // 3
    sources, results, held, sems = refs[:count], refs[count:2 * count], refs[2 * count:-1], refs[-1]
    loads = [pltpu.make_async_copy(sources[i], held[i], sems.at[0, i]) for i in range(count)]
    stores = [pltpu.make_async_copy(held[i], results[i], sems.at[1, i]) for i in range(count)]
    for load in loads:
        load.start()
    for load, store in zip(loads, stores):
        load.wait()
        store.start()
    for store in stores:
        store.wait()


def local(n, ndp, queries, keys, values, out_grad, out_weight, extents):
    rows, width = queries.shape
    per = HEADS // n
    assert per in (1, 2) and rows % 128 == 0
    span = per * HEAD
    padded = -(-span // 16) * 16
    seq = n * rows
    line = n // 2
    images = extents.shape[1]
    if span % 16:
        out_weight = lax.dynamic_slice_in_dim(
            out_weight, lax.axis_index("seq") * span, span, axis=0
        )
    vmem = pl.BlockSpec(memory_space=pltpu.VMEM)
    hbm = pl.BlockSpec(memory_space=pl.ANY)
    grad = jax.ShapeDtypeStruct((rows, width), BF16)
    weight = jax.ShapeDtypeStruct((span, width // ndp), F32)
    dma = pltpu.SemaphoreType.DMA
    buf = pltpu.VMEM
    parts = pl.pallas_call(
        functools.partial(kernel, n, ndp, images),
        out_shape=(grad, grad, grad, weight),
        in_specs=[pl.BlockSpec(memory_space=pltpu.SMEM), hbm, hbm, hbm, hbm, hbm],
        out_specs=(vmem, vmem, vmem, vmem),
        scratch_shapes=[
            buf((rows, width), BF16),
            buf((rows, width), BF16),
            buf((rows, width), BF16),
            buf((n, rows, width), BF16),
            buf((span, width), BF16),
            buf((3, width, rows), F32),
            buf((n, 3 * BAND, rows), BF16),
            buf((n, 3 * 64, rows), BF16),
            buf((n, 3 * BAND, rows), BF16),
            buf((n, 3 * 64, rows), BF16),
            buf((n, padded, rows), BF16),
            buf((n, padded, rows), BF16),
            buf((n, padded, rows), BF16),
            buf((n, padded, rows), BF16),
            buf((n, padded, rows), BF16),
            buf((n, padded, rows), BF16),
            buf((per, BAND, seq), BF16),
            buf((per, BAND, seq), BF16),
            buf((per, BAND, seq), BF16),
            buf((per, seq, BAND), BF16),
            buf((per, seq, BAND), BF16),
            buf((per, seq, seq), BF16),
            buf((per, 1, seq), F32),
            buf((padded, seq), F32),
            buf((per, BAND, seq), F32),
            buf((per, BAND, seq), F32),
            buf((ndp, padded, width // ndp), BF16),
            buf((ndp, padded, width // ndp), BF16),
        ]
        + [dma((n,))] * 10
        + [dma((n,)), dma((line,)), dma((line,)), dma((line,)), dma((ndp,)), dma((ndp,)), dma((5,))],
        compiler_params=pltpu.CompilerParams(
            collective_id=0, has_side_effects=True, vmem_limit_bytes=56 * 2**20
        ),
        cost_estimate=pl.CostEstimate(
            flops=10 * per * seq * seq * HEAD, bytes_accessed=10 * rows * width * 2,
            transcendentals=per * seq * seq,
        ),
    )(extents, queries, keys, values, out_grad, out_weight)
    return pl.pallas_call(
        finish,
        out_shape=(grad, grad, grad, weight),
        in_specs=[hbm] * 4,
        out_specs=(hbm, hbm, hbm, hbm),
        scratch_shapes=[buf(part.shape, part.dtype) for part in parts] + [dma((2, 4))],
        compiler_params=pltpu.CompilerParams(vmem_limit_bytes=56 * 2**20),
    )(*parts)


def solution(mesh):
    n, ndp = mesh.shape["seq"], mesh.shape["dp"]
    return jax.shard_map(
        functools.partial(local, n, ndp),
        mesh=mesh,
        in_specs=(
            P(("dp", "seq"), None),
            P(("dp", "seq"), None),
            P(("dp", "seq"), None),
            P(("dp", "seq"), None),
            P(),
            P("dp", None),
        ),
        out_specs=(
            P(("dp", "seq"), None),
            P(("dp", "seq"), None),
            P(("dp", "seq"), None),
            P("seq", "dp"),
        ),
        check_vma=False,
    )
```
